256 devices in a mesh: grp: 32 (over x, y, z_lo), tp: 8 (over z_hi, core).
Axes of the slice: x: 4, y: 4, z: 8 (z_hi: 4, z_lo: 2; z = z_hi * 2 + z_lo), core: 2. Of those that a mesh axis runs over, the one named last changes fastest.
Arguments:
- queries: bfloat16 [8192, 4096], P('grp', 'tp'), may hold values from -24 to 24
- suffix_kv: bfloat16 [8192, 2, 1024], P('grp', None, 'tp'), may hold values from -12 to 12
- prefix_cache: bfloat16 [32, 2, 1536, 1024], P('grp', None, None, 'tp'), may hold values from -20 to 20
- out_weight: bfloat16 [4096, 8192], P('tp'), may hold values from -0.5 to 0.5
- readers: int32 [32, 16], P('grp'), may hold values from 0 to 31, all different within a row
- owner: int32 [32], replicated, may hold values from 0 to 31, each once
- lengths: int32 [32, 16], P('grp'), may hold values from 1 to 20, 256 in all within a row
Outputs:
- mixed: bfloat16 [8192, 8192], P('grp', 'tp')
The draws below stay inside these ranges and needn't reach their ends.
Inputs may be any that keep to these rules, and one draw needn't show every extreme that they name: The 16 prefixes of one row of readers are different; every prefix is read by some device. `owner`: each grp device holds exactly one prefix. `lengths`: each row sums to 256 and its largest entry is 20.
All inputs are finite; a program needn't handle non-finite values.
Results may differ from the reference program's by a relative error of at most 0.025.
Values may be sent and summed in bfloat16 or wider, within the bound.
A program may use at most 128 MiB of HBM per device.

```python
import math
import jax
import jax.numpy as jnp
import numpy as np
from jax import lax

D = 8192
HEADS = 32
KV_HEADS = 8
HEAD = 128
PL = 1536
SEQS = 16
MOST = 20
SUF_DEV = 256
TOKENS = 8192
N_GRP = 32
N_TP = 8


def draw_queries(key, part):
    key = jax.random.fold_in(key, 11)
    key_normal = jax.random.fold_in(key, 0)
    per_group = HEADS // KV_HEADS
    values_drawn = jnp.clip(1.5 * jax.random.normal(key_normal, (TOKENS, KV_HEADS, per_group, HEAD), jnp.float32), -6.0, 6.0)
    return values_drawn.reshape(TOKENS, HEADS * HEAD).astype(jnp.bfloat16)


def draw_prefix_cache(key, part):
    key = jax.random.fold_in(key, 12)
    key_normal = jax.random.fold_in(key, 0)
    values_drawn = jnp.clip(jax.random.normal(key_normal, (N_GRP, 2, PL, KV_HEADS, HEAD), jnp.float32), -4.0, 4.0)
    return values_drawn.reshape(N_GRP, 2, PL, KV_HEADS * HEAD).astype(jnp.bfloat16)


def raised(entries, rng, source, target, blocks, factor):
    owner, partner = [(jnp.arange(entries.shape[axis_at]) // (entries.shape[axis_at] // blocks)).reshape([-1 if axis == axis_at else 1 for axis in range(entries.ndim)]) for axis_at in (source, target)]
    chosen = jax.random.permutation(rng, blocks)[partner]
    strong = (owner == chosen) | (owner == (partner + blocks // 2) % blocks)
    return jnp.where(strong, factor * entries, entries)


def steps_of(key, dims, cuts, low, top_value):
    def one(axis_at, blocks):
        draws = jax.random.uniform(jax.random.fold_in(jax.random.fold_in(key, 6), axis_at), (blocks,), jnp.float32, low / len(cuts), top_value / len(cuts))
        return jnp.repeat(jnp.exp(draws), dims[axis_at] // blocks).reshape((-1,) + (1,) * (len(dims) - axis_at - 1))

    factor_of = one(*cuts[0])
    for cut in cuts[1:]:
        factor_of = factor_of * one(*cut)
    return factor_of


def distinct(rng, rows, amount, top, lift):
    order = jax.random.permutation(jax.random.fold_in(rng, 1), amount)
    boost = order
    for power in range(3):
        boost = boost * boost // amount
    boost = boost * lift // amount
    chance = jax.random.randint(jax.random.fold_in(rng, 2), (rows, amount), 0, 4096) + boost
    sure = jax.random.permutation(jax.random.fold_in(rng, 3), rows)[jnp.arange(amount) % rows]
    chance = jnp.where(jnp.arange(rows)[:, None] == sure[None, :], 1 << 14, chance)
    score = chance * amount + jnp.arange(amount)
    return lax.top_k(score.astype(jnp.int32), top)[1].astype(jnp.int32)


def profile(amount, total, bound, slope):
    weights = [(1 << 20) // math.isqrt(standing ** slope) + 1 for standing in range(2, amount + 1)]
    surplus, holding = total - bound - (amount - 1), [1] * (amount - 1)
    while surplus > 0:
        free = [i for i in range(amount - 1) if holding[i] < bound]
        pool, remaining = sum([weights[i] for i in free]), surplus
        for i in free:
            extra = min(bound - holding[i], max(1, remaining * weights[i] // pool), surplus)
            holding[i] = holding[i] + extra
            surplus = surplus - extra
    return np.array([bound] + holding)


def uneven_parts(key, count, total, limit, skew):
    if count == 2:
        one = jax.random.randint(key, (), max(1, total - limit), min(limit, total - 1) + 1)
        return jnp.stack([one, total - one])
    sizes = jnp.asarray(profile(count, total, limit, skew), jnp.int32)
    twos = (count - 1) // 2
    source_of, sink = sizes[1:1 + 2 * twos:2], sizes[2:2 + 2 * twos:2]
    slack = jnp.minimum(source_of - 1, limit - sink)
    passed = jax.random.randint(jax.random.fold_in(key, 1), (twos,), 0, 1 << 20) % (slack + 1)
    sizes = sizes.at[1:1 + 2 * twos:2].set(source_of - passed).at[2:2 + 2 * twos:2].set(sink + passed)
    return sizes[jax.random.permutation(jax.random.fold_in(key, 2), count)]


def centred(key, extent, scale, limit, cuts=(), held_as=jnp.bfloat16):
    result = scale * jax.random.normal(key, extent, jnp.float32)
    if cuts:
        result = result * steps_of(key, extent, cuts, -0.22, 0.18)
    return jnp.clip(result, -limit, limit).astype(held_as)


def heavy_noise(key, shape, width, bound, pieces, heavy, kind=jnp.bfloat16):
    drawn = width * jax.random.normal(key, shape, jnp.float32)
    if pieces:
        drawn = drawn * steps_of(key, shape, pieces, -0.22, 0.18)
    return jnp.clip(raised(drawn, jax.random.fold_in(key, 3), *heavy), -bound, bound).astype(kind)


def setup_inputs(seed: int = 0) -> dict:
    splits = jax.random.split(jax.random.key(seed), 8)
    return {
        "queries": draw_queries(jax.random.fold_in(splits[7], 71), 0),
        "suffix_kv": centred(splits[1], (TOKENS, 2, KV_HEADS * HEAD), 2.0, 12.0, ((0, 32), (2, 8))),
        "prefix_cache": draw_prefix_cache(jax.random.fold_in(splits[7], 71), 0),
        "out_weight": heavy_noise(splits[3], (HEADS * HEAD, D), (HEADS * HEAD // 16) ** -0.5, 0.5, ((0, 8),), (0, 1, 8, 2.0)),
        "readers": distinct(splits[4], N_GRP, N_GRP, SEQS, 8192),
        "owner": jax.random.permutation(splits[5], N_GRP).astype(jnp.int32),
        "lengths": jax.vmap(lambda own: uneven_parts(own, SEQS, SUF_DEV, MOST, 1))(jax.random.split(splits[6], N_GRP)).reshape((N_GRP, SEQS)).astype(jnp.int32),
    }


NEG_FILL = -1e30


def rounded(values_in):
    return lax.optimization_barrier(values_in.astype(jnp.bfloat16)).astype(jnp.float32)


def reference(queries, suffix_kv, prefix_cache, out_weight, readers, owner, lengths):
    per_group = HEADS // KV_HEADS
    inv_root = HEAD ** -0.5
    query_all = queries.reshape(N_GRP, SUF_DEV, KV_HEADS, per_group, HEAD)
    suffix_all = suffix_kv.reshape(N_GRP, SUF_DEV, 2, KV_HEADS, HEAD)
    caches_split = prefix_cache.reshape(N_GRP, 2, PL, KV_HEADS, HEAD)
    column_count = HEADS * HEAD // N_TP
    weight_split = out_weight.reshape(N_TP, column_count, D)

    def one_device(operands):
        grouped, suffix_dev, reader_row, length_row = operands
        seq_ends = jnp.cumsum(length_row).astype(jnp.int32)
        seq_starts = (seq_ends - length_row).astype(jnp.int32)
        row_index = jnp.arange(SUF_DEV, dtype=jnp.int32)
        seq_of = jnp.sum((row_index[:, None] >= seq_ends[None, :]).astype(jnp.int32), axis=1).astype(jnp.int32)
        holders = owner[reader_row].astype(jnp.int32)
        padded = jnp.concatenate([grouped, jnp.zeros((MOST, KV_HEADS, per_group, HEAD), jnp.bfloat16)], axis=0)
        suffix_keys = suffix_dev[:, 0].astype(jnp.float32)
        suffix_values = suffix_dev[:, 1].astype(jnp.float32)

        def per_sequence(seq_id):
            first_row = seq_starts[seq_id]
            rows_query = lax.dynamic_slice_in_dim(padded, first_row, MOST, 0).astype(jnp.float32)
            holder = holders[seq_id]
            own_keys = caches_split[holder, 0].astype(jnp.float32)
            own_values = caches_split[holder, 1].astype(jnp.float32)
            prefix_scores = jnp.einsum("rkge,pke->rkgp", rows_query, own_keys) * inv_root
            suffix_scores = jnp.einsum("rkge,jke->rkgj", rows_query, suffix_keys) * inv_root
            visible = (seq_of[None, :] == seq_id) & (row_index[None, :] <= first_row + jnp.arange(MOST, dtype=jnp.int32)[:, None])
            suffix_scores = jnp.where(visible[:, None, None, :], suffix_scores, NEG_FILL)
            row_top = jnp.maximum(jnp.max(prefix_scores, axis=3), jnp.max(suffix_scores, axis=3))
            prefix_weights = jnp.exp(prefix_scores - row_top[..., None])
            suffix_weights = jnp.exp(suffix_scores - row_top[..., None])
            row_total = jnp.sum(prefix_weights, axis=3) + jnp.sum(suffix_weights, axis=3)
            weighted = jnp.einsum("rkgp,pke->rkge", rounded(prefix_weights), own_values)
            weighted = weighted + jnp.einsum("rkgj,jke->rkge", rounded(suffix_weights), suffix_values)
            return (weighted / row_total[..., None]).astype(jnp.bfloat16)

        results = lax.map(per_sequence, jnp.arange(SEQS, dtype=jnp.int32))
        flattened = results.reshape(SEQS * MOST, HEADS * HEAD)
        gather_rows = (seq_of * MOST + row_index - seq_starts[seq_of]).astype(jnp.int32)
        attention = flattened[gather_rows]
        summed = jnp.zeros((SUF_DEV, D), jnp.float32)
        for slot in range(N_TP):
            partial_term = jnp.dot(attention[:, slot * column_count:(slot + 1) * column_count], weight_split[slot], preferred_element_type=jnp.float32)
            summed = summed + partial_term.astype(jnp.bfloat16).astype(jnp.float32)
        return summed.astype(jnp.bfloat16)

    outputs = lax.map(one_device, (query_all, suffix_all, readers, lengths))
    return outputs.reshape(N_GRP * SUF_DEV, D)
```

```python
import math

import jax
import jax.numpy as jnp
from jax import lax
from jax.experimental import pallas as pl
from jax.experimental.pallas import tpu as pltpu
from jax.sharding import PartitionSpec as P

HEAD = 128
MOST = 20
MAIN = 16
TAIL = MOST - MAIN
PER = 4
SLOT = MOST * PER
NX, NY, NZ = 4, 4, 2
HOLDERS = NX * NY * NZ
GROUP = 8
NEG = -1e30
FACTOR = math.log2(math.e) / math.sqrt(HEAD)
F32 = jnp.float32
BF16 = jnp.bfloat16


def dot(a, b):
    return jnp.dot(a, b, preferred_element_type=F32)


def dot_t(a, b):
    return lax.dot_general(a, b, (((1,), (1,)), ((), ())), preferred_element_type=F32)


def shifted(x, y, z, d, sign):
    dx, dy, dz = d // (NY * NZ), (d // NZ) % NY, d % NZ
    if sign > 0:
        nx, ny, nz = (x + dx) % NX, (y + dy) % NY, (z + dz) % NZ
    else:
        nx, ny, nz = (x + NX - dx) % NX, (y + NY - dy) % NY, (z + NZ - dz) % NZ
    return nx * (NY * NZ) + ny * NZ + nz


def row_places(shape, axis, me, readers, owner, lengths):
    x, y, z = me
    rows = lax.broadcasted_iota(jnp.int32, shape, axis)
    slot = jnp.zeros(shape, jnp.int32)
    first = jnp.zeros(shape, jnp.int32)
    start = jnp.int32(0)
    for s in range(readers.shape[1]):
        holder = owner[readers[0, s]]
        hx, hy, hz = holder // (NY * NZ), (holder // NZ) % NY, holder % NZ
        d = ((hx + NX - x) % NX) * (NY * NZ) + ((hy + NY - y) % NY) * NZ + (hz + NZ - z) % NZ
        inside = rows >= start
        slot = jnp.where(inside, d, slot)
        first = jnp.where(inside, start, first)
        start = start + lengths[0, s]
    return rows, slot, rows - first, first


def one_hot(cond):
    return jnp.where(cond, 1.0, 0.0).astype(BF16)


def attend_kernel(
    q, kv, cache, readers, owner, lengths, out,
    send, recv, back, ret, lback, lret, sufw, suft,
    send_sem, recv_sem, back_sem, ret_sem, lback_sem, lret_sem,
):
    me = lax.axis_index("grp")
    x, y, z = me // (NY * NZ), (me // NZ) % NY, me % NZ
    rows_n = q.shape[0]

    barrier = pltpu.get_barrier_semaphore()

    def greet(d, carry):
        pl.semaphore_signal(
            barrier, inc=1, device_id={"grp": shifted(x, y, z, d, 1)},
            device_id_type=pl.DeviceIdType.MESH,
        )
        return carry

    lax.fori_loop(1, HOLDERS, greet, 0)

    _, slot, place, _ = row_places((1, rows_n), 1, (x, y, z), readers, owner, lengths)
    wide = lax.broadcasted_iota(jnp.int32, (HOLDERS * MAIN, rows_n), 0)
    main_at = jnp.where(place < MAIN, slot * MAIN + place, -1)
    main = dot(one_hot(wide == main_at), q[...]).astype(BF16)
    tail = jnp.zeros((HOLDERS * MAIN, HEAD), F32)
    for k in range(PER):
        cols = slice(k * HEAD, (k + 1) * HEAD)
        send[:, k * MAIN:(k + 1) * MAIN, :] = main[:, cols].reshape(HOLDERS, MAIN, HEAD)
        tail_at = jnp.where(place >= MAIN, slot * MAIN + TAIL * k + place - MAIN, -1)
        tail = tail + dot(one_hot(wide == tail_at), q[:, cols])
    send[:, PER * MAIN:, :] = tail.astype(BF16).reshape(HOLDERS, MAIN, HEAD)

    pl.semaphore_wait(barrier, HOLDERS - 1)

    def dispatch(d):
        return pltpu.make_async_remote_copy(
            src_ref=send.at[d], dst_ref=recv.at[d],
            send_sem=send_sem.at[d], recv_sem=recv_sem.at[d],
            device_id={"grp": shifted(x, y, z, d, 1)},
            device_id_type=pl.DeviceIdType.MESH,
        )

    def give(d):
        return pltpu.make_async_remote_copy(
            src_ref=back.at[d], dst_ref=ret.at[d],
            send_sem=back_sem.at[d], recv_sem=ret_sem.at[d],
            device_id={"grp": shifted(x, y, z, d, -1)},
            device_id_type=pl.DeviceIdType.MESH,
        )

    def give_l(d):
        return pltpu.make_async_remote_copy(
            src_ref=lback.at[d], dst_ref=lret.at[d],
            send_sem=lback_sem.at[d], recv_sem=lret_sem.at[d],
            device_id={"grp": shifted(x, y, z, d, -1)},
            device_id_type=pl.DeviceIdType.MESH,
        )

    def start_dispatch(d, carry):
        dispatch(d).start()
        return carry

    lax.fori_loop(1, HOLDERS, start_dispatch, 0)
    recv[0] = send[0]

    at, slot, place, first = row_places((rows_n, 1), 0, (x, y, z), readers, owner, lengths)
    other = lax.broadcasted_iota(jnp.int32, (rows_n, rows_n), 1)
    visible = (other >= first) & (other <= at)
    keys, values = kv[:, 0, :], kv[:, 1, :]
    for k in range(PER):
        s = dot_t(q[:, k * HEAD:(k + 1) * HEAD], keys)
        s = jnp.where(visible, s, NEG)
        top = jnp.max(s, axis=1, keepdims=True)
        w = jnp.exp2((s - top) * FACTOR)
        total = jnp.sum(w, axis=1, keepdims=True)
        sufw[k] = dot(w.astype(BF16), values)
        suft[k, :, 0:1] = top * FACTOR
        suft[k, :, 1:2] = total

    prefix_keys = cache[0, 0]
    prefix_values = jnp.concatenate(
        [cache[0, 1], jnp.ones((cache.shape[2], HEAD), BF16)], axis=1
    )
    lane = lax.broadcasted_iota(jnp.int32, (SLOT, HEAD), 1)
    sub = lax.broadcasted_iota(jnp.int32, (SLOT, HEAD), 0)
    for a in range(HOLDERS // GROUP):
        low = a * GROUP

        def wait_slot(d, carry):
            dispatch(d).wait_recv()
            return carry

        lax.fori_loop(max(low, 1), low + GROUP, wait_slot, 0)
        block = recv[low:low + GROUP].reshape(GROUP * SLOT, HEAD)
        s = dot_t(block, prefix_keys)
        top = jnp.max(s, axis=1, keepdims=True)
        w = jnp.exp2((s - top) * FACTOR)
        o = dot(w.astype(BF16), prefix_values)
        total = o[:, HEAD:]
        back[low:low + GROUP] = (o[:, :HEAD] / total).astype(BF16).reshape(GROUP, SLOT, HEAD)
        lse = top * FACTOR + jnp.log2(total)
        for i in range(GROUP):
            part = lse[i * SLOT:(i + 1) * SLOT]
            lback[low + i] = jnp.sum(jnp.where(lane == sub, part, 0.0), axis=0, keepdims=True)

        def start_give(d, carry):
            give(d).start()
            give_l(d).start()
            return carry

        lax.fori_loop(max(low, 1), low + GROUP, start_give, 0)

    ret[0] = back[0]
    lret[0] = lback[0]

    cols = lax.broadcasted_iota(jnp.int32, (rows_n, HOLDERS * MAIN), 1)
    from_main = one_hot(cols == jnp.where(place < MAIN, slot * MAIN + place, -1))
    slots = lax.broadcasted_iota(jnp.int32, (rows_n, HOLDERS), 1)
    from_slot = one_hot(slots == slot)
    lanes = lax.broadcasted_iota(jnp.int32, (rows_n, HEAD), 1)

    def wait_ret(d, carry):
        give(d).wait_recv()
        give_l(d).wait_recv()
        return carry

    lax.fori_loop(1, HOLDERS, wait_ret, 0)

    l_all = lret[...].reshape(HOLDERS, HEAD)
    l_high = l_all.astype(BF16)
    l_rest = l_all - l_high.astype(F32)
    l_mid = l_rest.astype(BF16)
    l_low = (l_rest - l_mid.astype(F32)).astype(BF16)
    l_rows = dot(from_slot, l_high) + dot(from_slot, l_mid) + dot(from_slot, l_low)
    tails = ret[:, PER * MAIN:, :].reshape(HOLDERS * MAIN, HEAD)
    for k in range(PER):
        from_tail = one_hot(
            cols == jnp.where(place >= MAIN, slot * MAIN + TAIL * k + place - MAIN, -1)
        )
        mains = ret[:, k * MAIN:(k + 1) * MAIN, :].reshape(HOLDERS * MAIN, HEAD)
        pre = dot(from_main, mains) + dot(from_tail, tails)
        l_at = jnp.where(place < MAIN, MAIN * k + place, MAIN * PER + TAIL * k + place - MAIN)
        l_pre = jnp.sum(jnp.where(lanes == l_at, l_rows, 0.0), axis=1, keepdims=True)
        l_suf = suft[k, :, 0:1]
        top = jnp.maximum(l_pre, l_suf)
        pre_f, suf_f = jnp.exp2(l_pre - top), jnp.exp2(l_suf - top)
        total = pre_f + suf_f * suft[k, :, 1:2]
        out[:, k * HEAD:(k + 1) * HEAD] = (
            (pre * pre_f + sufw[k] * suf_f) / total
        ).astype(BF16)

    def finish(d, carry):
        dispatch(d).wait_send()
        give(d).wait_send()
        give_l(d).wait_send()
        return carry

    lax.fori_loop(1, HOLDERS, finish, 0)


def attend(queries, suffix_kv, cache, readers, owner, lengths):
    rows_n = queries.shape[0]
    vmem = pl.BlockSpec(memory_space=pltpu.VMEM)
    smem = pl.BlockSpec(memory_space=pltpu.SMEM)
    dma = pltpu.SemaphoreType.DMA((HOLDERS,))
    slots = pltpu.VMEM((HOLDERS, SLOT, HEAD), BF16)
    lses = pltpu.VMEM((HOLDERS, 1, HEAD), F32)
    return pl.pallas_call(
        attend_kernel,
        out_shape=jax.ShapeDtypeStruct(queries.shape, BF16),
        in_specs=[vmem, vmem, vmem, smem, smem, smem],
        out_specs=vmem,
        scratch_shapes=[
            slots, slots, slots, slots, lses, lses,
            pltpu.VMEM((PER, rows_n, HEAD), F32),
            pltpu.VMEM((PER, rows_n, HEAD), F32),
            dma, dma, dma, dma, dma, dma,
        ],
        compiler_params=pltpu.CompilerParams(
            collective_id=0, has_side_effects=True, vmem_limit_bytes=56 * 1024 * 1024
        ),
        cost_estimate=pl.CostEstimate(
            flops=4 * HOLDERS * SLOT * cache.shape[2] * HEAD,
            bytes_accessed=4 * 1024 * 1024,
            transcendentals=HOLDERS * SLOT * cache.shape[2],
        ),
        name="attend",
    )(queries, suffix_kv, cache, readers, owner, lengths)


def local(queries, suffix_kv, prefix_cache, out_weight, readers, owner, lengths):
    attention = attend(queries, suffix_kv, prefix_cache, readers, owner, lengths)
    partial = jnp.dot(attention, out_weight, preferred_element_type=F32)
    return lax.psum_scatter(partial.astype(BF16), "tp", scatter_dimension=1, tiled=True)


def solution(mesh):
    return jax.shard_map(
        local,
        mesh=mesh,
        in_specs=(
            P("grp", "tp"),
            P("grp", None, "tp"),
            P("grp", None, None, "tp"),
            P("tp", None),
            P("grp", None),
            P(),
            P("grp", None),
        ),
        out_specs=P("grp", "tp"),
        check_vma=False,
    )
```

```python
import math

import jax
import jax.numpy as jnp
from jax import lax
from jax.experimental import pallas as pl
from jax.experimental.pallas import tpu as pltpu
from jax.sharding import PartitionSpec as P

HEAD = 128
MOST = 20
MAIN = 16
TAIL = MOST - MAIN
PER = 4
SLOT = MOST * PER
NX, NY, NZ = 4, 4, 2
HOLDERS = NX * NY * NZ
GROUP = 8
RING = 4
CORES = 2
HOPS = RING - 1
PIECES = 4
NEG = -1e30
FACTOR = math.log2(math.e) / math.sqrt(HEAD)
F32 = jnp.float32
BF16 = jnp.bfloat16


def dot(a, b):
    return jnp.dot(a, b, preferred_element_type=F32)


def dot_t(a, b):
    return lax.dot_general(a, b, (((1,), (1,)), ((), ())), preferred_element_type=F32)


def shifted(x, y, z, d, sign):
    dx, dy, dz = d // (NY * NZ), (d // NZ) % NY, d % NZ
    if sign > 0:
        nx, ny, nz = (x + dx) % NX, (y + dy) % NY, (z + dz) % NZ
    else:
        nx, ny, nz = (x + NX - dx) % NX, (y + NY - dy) % NY, (z + NZ - dz) % NZ
    return nx * (NY * NZ) + ny * NZ + nz


def row_places(shape, axis, me, readers, owner, lengths):
    x, y, z = me
    rows = lax.broadcasted_iota(jnp.int32, shape, axis)
    slot = jnp.zeros(shape, jnp.int32)
    first = jnp.zeros(shape, jnp.int32)
    start = jnp.int32(0)
    for s in range(readers.shape[1]):
        holder = owner[readers[0, s]]
        hx, hy, hz = holder // (NY * NZ), (holder // NZ) % NY, holder % NZ
        d = ((hx + NX - x) % NX) * (NY * NZ) + ((hy + NY - y) % NY) * NZ + (hz + NZ - z) % NZ
        inside = rows >= start
        slot = jnp.where(inside, d, slot)
        first = jnp.where(inside, start, first)
        start = start + lengths[0, s]
    return rows, slot, rows - first, first


def one_hot(cond):
    return jnp.where(cond, 1.0, 0.0).astype(BF16)


def attend_kernel(
    q, kv, cache, weight, readers, owner, lengths, out,
    send, recv, back, ret, lback, lret, sufw, suft,
    w_own, w_sib, att, att_sib, part, going, coming,
    send_sem, recv_sem, back_sem, ret_sem, lback_sem, lret_sem,
    own_sem, sib_send, sib_recv, att_send, att_recv, go_sem, come_sem,
):
    me = lax.axis_index("grp")
    x, y, z = me // (NY * NZ), (me // NZ) % NY, me % NZ
    tp = lax.axis_index("tp")
    h, core = tp // CORES, tp % CORES
    sibling = h * CORES + 1 - core
    beside = [((h + 1) % RING) * CORES + core, ((h + RING - 1) % RING) * CORES + core]
    rows_n = q.shape[0]
    wide_out = out.shape[1]

    barrier = pltpu.get_barrier_semaphore()

    def greet(d, carry):
        pl.semaphore_signal(
            barrier, inc=1, device_id={"grp": shifted(x, y, z, d, 1)},
            device_id_type=pl.DeviceIdType.MESH,
        )
        return carry

    lax.fori_loop(1, HOLDERS, greet, 0)
    for partner in [sibling] + beside:
        pl.semaphore_signal(
            barrier, inc=1, device_id={"tp": partner}, device_id_type=pl.DeviceIdType.MESH
        )

    def columns(b, of_core):
        return pl.ds(pl.multiple_of((b * CORES + of_core) * wide_out, wide_out), wide_out)

    def fetch(b):
        return pltpu.make_async_copy(weight.at[:, columns(b, core)], w_own.at[b], own_sem.at[b])

    def swap(b):
        return pltpu.make_async_remote_copy(
            src_ref=weight.at[:, columns(b, 1 - core)], dst_ref=w_sib.at[b],
            send_sem=sib_send.at[b], recv_sem=sib_recv.at[b],
            device_id={"tp": sibling}, device_id_type=pl.DeviceIdType.MESH,
        )

    for b in range(RING):
        fetch(b).start()

    _, slot, place, _ = row_places((1, rows_n), 1, (x, y, z), readers, owner, lengths)
    wide = lax.broadcasted_iota(jnp.int32, (HOLDERS * MAIN, rows_n), 0)
    main_at = jnp.where(place < MAIN, slot * MAIN + place, -1)
    main = dot(one_hot(wide == main_at), q[...]).astype(BF16)
    tail = jnp.zeros((HOLDERS * MAIN, HEAD), F32)
    for k in range(PER):
        cols = slice(k * HEAD, (k + 1) * HEAD)
        send[:, k * MAIN:(k + 1) * MAIN, :] = main[:, cols].reshape(HOLDERS, MAIN, HEAD)
        tail_at = jnp.where(place >= MAIN, slot * MAIN + TAIL * k + place - MAIN, -1)
        tail = tail + dot(one_hot(wide == tail_at), q[:, cols])
    send[:, PER * MAIN:, :] = tail.astype(BF16).reshape(HOLDERS, MAIN, HEAD)

    pl.semaphore_wait(barrier, HOLDERS - 1 + 3)

    def dispatch(d):
        return pltpu.make_async_remote_copy(
            src_ref=send.at[d], dst_ref=recv.at[d],
            send_sem=send_sem.at[d], recv_sem=recv_sem.at[d],
            device_id={"grp": shifted(x, y, z, d, 1)},
            device_id_type=pl.DeviceIdType.MESH,
        )

    def give(d):
        return pltpu.make_async_remote_copy(
            src_ref=back.at[d], dst_ref=ret.at[d],
            send_sem=back_sem.at[d], recv_sem=ret_sem.at[d],
            device_id={"grp": shifted(x, y, z, d, -1)},
            device_id_type=pl.DeviceIdType.MESH,
        )

    def give_l(d):
        return pltpu.make_async_remote_copy(
            src_ref=lback.at[d], dst_ref=lret.at[d],
            send_sem=lback_sem.at[d], recv_sem=lret_sem.at[d],
            device_id={"grp": shifted(x, y, z, d, -1)},
            device_id_type=pl.DeviceIdType.MESH,
        )

    def start_dispatch(d, carry):
        dispatch(d).start()
        return carry

    lax.fori_loop(1, HOLDERS, start_dispatch, 0)
    recv[0] = send[0]
    for b in range(RING):
        swap(b).start()

    at, slot, place, first = row_places((rows_n, 1), 0, (x, y, z), readers, owner, lengths)
    other = lax.broadcasted_iota(jnp.int32, (rows_n, rows_n), 1)
    visible = (other >= first) & (other <= at)
    keys, values = kv[:, 0, :], kv[:, 1, :]
    for k in range(PER):
        s = dot_t(q[:, k * HEAD:(k + 1) * HEAD], keys)
        s = jnp.where(visible, s, NEG)
        top = jnp.max(s, axis=1, keepdims=True)
        w = jnp.exp2((s - top) * FACTOR)
        total = jnp.sum(w, axis=1, keepdims=True)
        sufw[k] = dot(w.astype(BF16), values)
        suft[k, :, 0:1] = top * FACTOR
        suft[k, :, 1:2] = total

    prefix_keys = cache[0, 0]
    prefix_values = jnp.concatenate(
        [cache[0, 1], jnp.ones((cache.shape[2], HEAD), BF16)], axis=1
    )
    lane = lax.broadcasted_iota(jnp.int32, (SLOT, HEAD), 1)
    sub = lax.broadcasted_iota(jnp.int32, (SLOT, HEAD), 0)
    for a in range(HOLDERS // GROUP):
        low = a * GROUP

        def wait_slot(d, carry):
            dispatch(d).wait_recv()
            return carry

        lax.fori_loop(max(low, 1), low + GROUP, wait_slot, 0)
        block = recv[low:low + GROUP].reshape(GROUP * SLOT, HEAD)
        s = dot_t(block, prefix_keys)
        top = jnp.max(s, axis=1, keepdims=True)
        w = jnp.exp2((s - top) * FACTOR)
        o = dot(w.astype(BF16), prefix_values)
        total = o[:, HEAD:]
        back[low:low + GROUP] = (o[:, :HEAD] / total).astype(BF16).reshape(GROUP, SLOT, HEAD)
        lse = top * FACTOR + jnp.log2(total)
        for i in range(GROUP):
            piece_l = lse[i * SLOT:(i + 1) * SLOT]
            lback[low + i] = jnp.sum(jnp.where(lane == sub, piece_l, 0.0), axis=0, keepdims=True)

        def start_give(d, carry):
            give(d).start()
            give_l(d).start()
            return carry

        lax.fori_loop(max(low, 1), low + GROUP, start_give, 0)

    ret[0] = back[0]
    lret[0] = lback[0]

    cols = lax.broadcasted_iota(jnp.int32, (rows_n, HOLDERS * MAIN), 1)
    from_main = one_hot(cols == jnp.where(place < MAIN, slot * MAIN + place, -1))
    slots = lax.broadcasted_iota(jnp.int32, (rows_n, HOLDERS), 1)
    from_slot = one_hot(slots == slot)
    lanes = lax.broadcasted_iota(jnp.int32, (rows_n, HEAD), 1)

    def wait_ret(d, carry):
        give(d).wait_recv()
        give_l(d).wait_recv()
        return carry

    lax.fori_loop(1, HOLDERS, wait_ret, 0)

    l_all = lret[...].reshape(HOLDERS, HEAD)
    l_high = l_all.astype(BF16)
    l_rest = l_all - l_high.astype(F32)
    l_mid = l_rest.astype(BF16)
    l_low = (l_rest - l_mid.astype(F32)).astype(BF16)
    l_rows = dot(from_slot, l_high) + dot(from_slot, l_mid) + dot(from_slot, l_low)
    tails = ret[:, PER * MAIN:, :].reshape(HOLDERS * MAIN, HEAD)
    for k in range(PER):
        from_tail = one_hot(
            cols == jnp.where(place >= MAIN, slot * MAIN + TAIL * k + place - MAIN, -1)
        )
        mains = ret[:, k * MAIN:(k + 1) * MAIN, :].reshape(HOLDERS * MAIN, HEAD)
        pre = dot(from_main, mains) + dot(from_tail, tails)
        l_at = jnp.where(place < MAIN, MAIN * k + place, MAIN * PER + TAIL * k + place - MAIN)
        l_pre = jnp.sum(jnp.where(lanes == l_at, l_rows, 0.0), axis=1, keepdims=True)
        l_suf = suft[k, :, 0:1]
        top = jnp.maximum(l_pre, l_suf)
        pre_f, suf_f = jnp.exp2(l_pre - top), jnp.exp2(l_suf - top)
        total = pre_f + suf_f * suft[k, :, 1:2]
        att[:, k * HEAD:(k + 1) * HEAD] = (
            (pre * pre_f + sufw[k] * suf_f) / total
        ).astype(BF16)

    share = pltpu.make_async_remote_copy(
        src_ref=att, dst_ref=att_sib, send_sem=att_send, recv_sem=att_recv,
        device_id={"tp": sibling}, device_id_type=pl.DeviceIdType.MESH,
    )
    share.start()
    for b in range(RING):
        fetch(b).wait()
        swap(b).wait()
    share.wait()

    half = rows_n // 2
    piece = half // PIECES

    def project(b, low, count):
        rows = slice(low, low + count)
        return dot(att[rows, :], w_own[b]) + dot(att_sib[rows, :], w_sib[b])

    def hop(way, step, i):
        return pltpu.make_async_remote_copy(
            src_ref=going.at[way, step, i], dst_ref=coming.at[way, step, i],
            send_sem=go_sem.at[way, step, i], recv_sem=come_sem.at[way, step, i],
            device_id={"tp": beside[way]}, device_id_type=pl.DeviceIdType.MESH,
        )

    before, after, across = (h + RING - 1) % RING, (h + 1) % RING, (h + 2) % RING
    for way, b in ((0, before), (1, after)):
        first_part = project(b, way * half, half).astype(BF16)
        for i in range(PIECES):
            going[way, 0, i] = first_part[i * piece:(i + 1) * piece]
            hop(way, 0, i).start()
    part[0] = project(across, 0, rows_n)
    part[1, :half] = project(after, 0, half)
    part[1, half:] = project(before, half, half)
    part[2] = project(h, 0, rows_n)
    for step in range(HOPS):
        for i in range(PIECES):
            for way in range(2):
                hop(way, step, i).wait_recv()
                low = way * half + i * piece
                total = coming[way, step, i].astype(F32) + part[step, low:low + piece]
                if step < HOPS - 1:
                    going[way, step + 1, i] = total.astype(BF16)
                    hop(way, step + 1, i).start()
                else:
                    out[low:low + piece] = total.astype(BF16)
    for way in range(2):
        for step in range(HOPS):
            for i in range(PIECES):
                hop(way, step, i).wait_send()

    def finish(d, carry):
        dispatch(d).wait_send()
        give(d).wait_send()
        give_l(d).wait_send()
        return carry

    lax.fori_loop(1, HOLDERS, finish, 0)


def attend(queries, suffix_kv, cache, weight, readers, owner, lengths):
    rows_n, width = queries.shape
    wide_out = weight.shape[1] // (RING * CORES)
    moved = pltpu.VMEM((2, HOPS, PIECES, rows_n // 2 // PIECES, wide_out), BF16)
    moved_sem = pltpu.SemaphoreType.DMA((2, HOPS, PIECES))
    block_sem = pltpu.SemaphoreType.DMA((RING,))
    vmem = pl.BlockSpec(memory_space=pltpu.VMEM)
    smem = pl.BlockSpec(memory_space=pltpu.SMEM)
    dma = pltpu.SemaphoreType.DMA((HOLDERS,))
    slots = pltpu.VMEM((HOLDERS, SLOT, HEAD), BF16)
    lses = pltpu.VMEM((HOLDERS, 1, HEAD), F32)
    return pl.pallas_call(
        attend_kernel,
        out_shape=jax.ShapeDtypeStruct((rows_n, wide_out), BF16),
        in_specs=[vmem, vmem, vmem, pl.BlockSpec(memory_space=pl.ANY), smem, smem, smem],
        out_specs=vmem,
        scratch_shapes=[
            slots, slots, slots, slots, lses, lses,
            pltpu.VMEM((PER, rows_n, HEAD), F32),
            pltpu.VMEM((PER, rows_n, HEAD), F32),
            pltpu.VMEM((RING, width, wide_out), BF16),
            pltpu.VMEM((RING, width, wide_out), BF16),
            pltpu.VMEM((rows_n, width), BF16),
            pltpu.VMEM((rows_n, width), BF16),
            pltpu.VMEM((HOPS, rows_n, wide_out), F32),
            moved, moved,
            dma, dma, dma, dma, dma, dma,
            block_sem, block_sem, block_sem,
            pltpu.SemaphoreType.DMA, pltpu.SemaphoreType.DMA,
            moved_sem, moved_sem,
        ],
        compiler_params=pltpu.CompilerParams(
            collective_id=0, has_side_effects=True, vmem_limit_bytes=56 * 1024 * 1024
        ),
        cost_estimate=pl.CostEstimate(
            flops=4 * HOLDERS * SLOT * cache.shape[2] * HEAD,
            bytes_accessed=4 * 1024 * 1024,
            transcendentals=HOLDERS * SLOT * cache.shape[2],
        ),
        name="attend",
    )(queries, suffix_kv, cache, weight, readers, owner, lengths)


def local(queries, suffix_kv, prefix_cache, out_weight, readers, owner, lengths):
    return attend(queries, suffix_kv, prefix_cache, out_weight, readers, owner, lengths)


def solution(mesh):
    return jax.shard_map(
        local,
        mesh=mesh,
        in_specs=(
            P("grp", "tp"),
            P("grp", None, "tp"),
            P("grp", None, None, "tp"),
            P("tp", None),
            P("grp", None),
            P(),
            P("grp", None),
        ),
        out_specs=P("grp", "tp"),
        check_vma=False,
    )
```

```python
import math

import jax
import jax.numpy as jnp
from jax import lax
from jax.experimental import pallas as pl
from jax.experimental.pallas import tpu as pltpu
from jax.sharding import PartitionSpec as P

HEAD = 128
MOST = 20
MAIN = 16
TAIL = MOST - MAIN
PER = 4
SLOT = MOST * PER
NX, NY, NZ = 4, 4, 2
HOLDERS = NX * NY * NZ
GROUP = 8
RING = 4
CORES = 2
PIECES = 4
HALVES = 2
CHIPS = RING * NZ
SHARE = 32
NEG = -1e30
FACTOR = math.log2(math.e) / math.sqrt(HEAD)
F32 = jnp.float32
BF16 = jnp.bfloat16


def dot(a, b):
    return jnp.dot(a, b, preferred_element_type=F32)


def dot_t(a, b):
    return lax.dot_general(a, b, (((1,), (1,)), ((), ())), preferred_element_type=F32)


def shifted(x, y, z, d, sign):
    dx, dy, dz = d // (NY * NZ), (d // NZ) % NY, d % NZ
    if sign > 0:
        nx, ny, nz = (x + dx) % NX, (y + dy) % NY, (z + dz) % NZ
    else:
        nx, ny, nz = (x + NX - dx) % NX, (y + NY - dy) % NY, (z + NZ - dz) % NZ
    return nx * (NY * NZ) + ny * NZ + nz


def row_places(shape, axis, me, readers, owner, lengths):
    x, y, z = me
    rows = lax.broadcasted_iota(jnp.int32, shape, axis)
    slot = jnp.zeros(shape, jnp.int32)
    first = jnp.zeros(shape, jnp.int32)
    start = jnp.int32(0)
    for s in range(readers.shape[1]):
        holder = owner[readers[0, s]]
        hx, hy, hz = holder // (NY * NZ), (holder // NZ) % NY, holder % NZ
        d = ((hx + NX - x) % NX) * (NY * NZ) + ((hy + NY - y) % NY) * NZ + (hz + NZ - z) % NZ
        inside = rows >= start
        slot = jnp.where(inside, d, slot)
        first = jnp.where(inside, start, first)
        start = start + lengths[0, s]
    return rows, slot, rows - first, first


def one_hot(cond):
    return jnp.where(cond, 1.0, 0.0).astype(BF16)


def attend_kernel(
    q, kv, cache, weight, readers, owner, lengths, out,
    send, recv, back, ret, lback, lret, sufw, suft,
    w_own, w_far, att, acc, ship, got,
    send_sem, recv_sem, back_sem, ret_sem, lback_sem, lret_sem,
    own_sem, sib_send, sib_recv, far_send, far_recv, ring_send, ring_recv,
    hop_send, hop_recv, core_send, core_recv, ship_send, ship_recv,
):
    me = lax.axis_index("grp")
    x, y, z = me // (NY * NZ), (me // NZ) % NY, me % NZ
    tp = lax.axis_index("tp")
    h, core = tp // CORES, tp % CORES
    sibling = h * CORES + 1 - core
    side = 1 - 2 * z
    partner = x * (NY * NZ) + y * NZ + 1 - z
    outer = (h * NZ + z + CHIPS - side) % CHIPS
    chip = [
        {"grp": partner, "tp": tp},
        {"grp": x * (NY * NZ) + y * NZ + outer % NZ, "tp": (outer // NZ) * CORES + core},
    ]
    rows_n = q.shape[0]
    wide_out = out.shape[1]
    pair_out = wide_out // NZ
    half_out = pair_out // HALVES

    barrier = pltpu.get_barrier_semaphore()

    def greet(d, carry):
        pl.semaphore_signal(
            barrier, inc=1, device_id={"grp": shifted(x, y, z, d, 1)},
            device_id_type=pl.DeviceIdType.MESH,
        )
        return carry

    lax.fori_loop(1, HOLDERS, greet, 0)
    for d in range(1, RING * CORES):
        pl.semaphore_signal(
            barrier, inc=1, device_id={"tp": (tp + d) % (RING * CORES)},
            device_id_type=pl.DeviceIdType.MESH,
        )

    pl.semaphore_signal(
        barrier, inc=1, device_id=chip[1], device_id_type=pl.DeviceIdType.MESH
    )

    def columns(b, of_core):
        return pl.multiple_of((b * CORES + of_core) * wide_out + z * pair_out, pair_out)

    def to(device, src, dst, send, recv):
        return pltpu.make_async_remote_copy(
            src_ref=src, dst_ref=dst, send_sem=send, recv_sem=recv,
            device_id=device, device_id_type=pl.DeviceIdType.MESH,
        )

    fetch_own = pltpu.make_async_copy(
        weight.at[:, pl.ds(columns(h, core), pair_out)], w_own.at[0], own_sem
    )
    fetch_own.start()
    give_own = to(
        {"tp": sibling}, weight.at[:, pl.ds(columns(h, 1 - core), pair_out)], w_own.at[1],
        sib_send, sib_recv,
    )
    cores = (core, 1 - core)

    def far(j, r, half):
        target = (h + RING - side * j) % RING
        rows = pl.ds(pl.multiple_of((x * NY + y) * SHARE, SHARE), SHARE)
        first = pl.multiple_of(columns(target, cores[r]) + half * half_out, half_out)
        return to(
            {"tp": target * CORES + cores[r]}, weight.at[rows, pl.ds(first, half_out)],
            w_far.at[half, (j - 1) * CORES + r, x, y],
            far_send.at[j - 1, r, half], far_recv.at[j - 1, r, half],
        )

    def ring(half, second, stage, way):
        step = 1 if way == 0 else 3
        back_by = (3 if way == 0 else 1) * stage
        along_x = (half == 0) == (second == 1)
        if along_x:
            bx, by = (x + back_by) % NX, y
            target = ((x + step) % NX) * (NY * NZ) + y * NZ + z
        else:
            bx, by = x, (y + back_by) % NY
            target = x * (NY * NZ) + ((y + step) % NY) * NZ + z
        some = pl.ds(2 * way, 2)
        if second == 0:
            block = w_far.at[half, :, bx, by]
            if stage == 1:
                block = w_far.at[half, :, bx, by, pl.ds(way * (SHARE // 2), SHARE // 2)]
        elif along_x:
            block = w_far.at[half, :, bx, some] if stage == 1 else w_far.at[half, :, bx]
        else:
            block = w_far.at[half, :, some, by] if stage == 1 else w_far.at[half, :, :, by]
        return to(
            {"grp": target}, block, block,
            ring_send.at[half, second, stage, way], ring_recv.at[half, second, stage, way],
        )

    ways = [(half, way) for half in range(HALVES) for way in range(2)]

    def ring_start(second, stage):
        for half, way in ways:
            ring(half, second, stage, way).start()

    def ring_wait(second, stage):
        for half, way in ways:
            ring(half, second, stage, way).wait_recv()

    shares = [
        (j, r, half) for j in range(1, RING) for r in range(CORES) for half in range(HALVES)
    ]

    _, slot, place, _ = row_places((1, rows_n), 1, (x, y, z), readers, owner, lengths)
    wide = lax.broadcasted_iota(jnp.int32, (HOLDERS * MAIN, rows_n), 0)
    main_at = jnp.where(place < MAIN, slot * MAIN + place, -1)
    main = dot(one_hot(wide == main_at), q[...]).astype(BF16)
    tail = jnp.zeros((HOLDERS * MAIN, HEAD), F32)
    for k in range(PER):
        cols = slice(k * HEAD, (k + 1) * HEAD)
        send[:, k * MAIN:(k + 1) * MAIN, :] = main[:, cols].reshape(HOLDERS, MAIN, HEAD)
        tail_at = jnp.where(place >= MAIN, slot * MAIN + TAIL * k + place - MAIN, -1)
        tail = tail + dot(one_hot(wide == tail_at), q[:, cols])
    send[:, PER * MAIN:, :] = tail.astype(BF16).reshape(HOLDERS, MAIN, HEAD)

    pl.semaphore_wait(barrier, HOLDERS - 1 + RING * CORES)

    def dispatch(d):
        return pltpu.make_async_remote_copy(
            src_ref=send.at[d], dst_ref=recv.at[d],
            send_sem=send_sem.at[d], recv_sem=recv_sem.at[d],
            device_id={"grp": shifted(x, y, z, d, 1)},
            device_id_type=pl.DeviceIdType.MESH,
        )

    def give(d):
        return pltpu.make_async_remote_copy(
            src_ref=back.at[d], dst_ref=ret.at[d],
            send_sem=back_sem.at[d], recv_sem=ret_sem.at[d],
            device_id={"grp": shifted(x, y, z, d, -1)},
            device_id_type=pl.DeviceIdType.MESH,
        )

    def give_l(d):
        return pltpu.make_async_remote_copy(
            src_ref=lback.at[d], dst_ref=lret.at[d],
            send_sem=lback_sem.at[d], recv_sem=lret_sem.at[d],
            device_id={"grp": shifted(x, y, z, d, -1)},
            device_id_type=pl.DeviceIdType.MESH,
        )

    def start_dispatch(d, carry):
        dispatch(d).start()
        return carry

    lax.fori_loop(1, HOLDERS, start_dispatch, 0)
    recv[0] = send[0]
    for j, r, half in shares:
        far(j, r, half).start()
    give_own.start()

    at, slot, place, first = row_places((rows_n, 1), 0, (x, y, z), readers, owner, lengths)
    other = lax.broadcasted_iota(jnp.int32, (rows_n, rows_n), 1)
    visible = (other >= first) & (other <= at)
    keys, values = kv[:, 0, :], kv[:, 1, :]
    for k in range(PER):
        s = dot_t(q[:, k * HEAD:(k + 1) * HEAD], keys)
        s = jnp.where(visible, s, NEG)
        top = jnp.max(s, axis=1, keepdims=True)
        w = jnp.exp2((s - top) * FACTOR)
        total = jnp.sum(w, axis=1, keepdims=True)
        sufw[k] = dot(w.astype(BF16), values)
        suft[k, :, 0:1] = top * FACTOR
        suft[k, :, 1:2] = total

    prefix_keys = cache[0, 0]
    prefix_values = jnp.concatenate(
        [cache[0, 1], jnp.ones((cache.shape[2], HEAD), BF16)], axis=1
    )
    lane = lax.broadcasted_iota(jnp.int32, (SLOT, HEAD), 1)
    sub = lax.broadcasted_iota(jnp.int32, (SLOT, HEAD), 0)
    for a in range(HOLDERS // GROUP):
        low = a * GROUP

        def wait_slot(d, carry):
            dispatch(d).wait_recv()
            return carry

        lax.fori_loop(max(low, 1), low + GROUP, wait_slot, 0)
        block = recv[low:low + GROUP].reshape(GROUP * SLOT, HEAD)
        s = dot_t(block, prefix_keys)
        top = jnp.max(s, axis=1, keepdims=True)
        w = jnp.exp2((s - top) * FACTOR)
        o = dot(w.astype(BF16), prefix_values)
        total = o[:, HEAD:]
        back[low:low + GROUP] = (o[:, :HEAD] / total).astype(BF16).reshape(GROUP, SLOT, HEAD)
        lse = top * FACTOR + jnp.log2(total)
        for i in range(GROUP):
            piece_l = lse[i * SLOT:(i + 1) * SLOT]
            lback[low + i] = jnp.sum(jnp.where(lane == sub, piece_l, 0.0), axis=0, keepdims=True)

        def start_give(d, carry):
            give(d).start()
            give_l(d).start()
            return carry

        lax.fori_loop(max(low, 1), low + GROUP, start_give, 0)
        if a == 1:
            for j, r, half in shares:
                far(j, r, half).wait_recv()
            ring_start(0, 0)
        if a == 3:
            ring_wait(0, 0)
            ring_start(0, 1)

    ret[0] = back[0]
    lret[0] = lback[0]

    cols = lax.broadcasted_iota(jnp.int32, (rows_n, HOLDERS * MAIN), 1)
    from_main = one_hot(cols == jnp.where(place < MAIN, slot * MAIN + place, -1))
    slots = lax.broadcasted_iota(jnp.int32, (rows_n, HOLDERS), 1)
    from_slot = one_hot(slots == slot)
    lanes = lax.broadcasted_iota(jnp.int32, (rows_n, HEAD), 1)

    def wait_ret(d, carry):
        give(d).wait_recv()
        give_l(d).wait_recv()
        return carry

    lax.fori_loop(1, HOLDERS, wait_ret, 0)
    ring_wait(0, 1)
    ring_start(1, 0)

    l_all = lret[...].reshape(HOLDERS, HEAD)
    l_high = l_all.astype(BF16)
    l_rest = l_all - l_high.astype(F32)
    l_mid = l_rest.astype(BF16)
    l_low = (l_rest - l_mid.astype(F32)).astype(BF16)
    l_rows = dot(from_slot, l_high) + dot(from_slot, l_mid) + dot(from_slot, l_low)
    tails = ret[:, PER * MAIN:, :].reshape(HOLDERS * MAIN, HEAD)
    for k in range(PER):
        from_tail = one_hot(
            cols == jnp.where(place >= MAIN, slot * MAIN + TAIL * k + place - MAIN, -1)
        )
        mains = ret[:, k * MAIN:(k + 1) * MAIN, :].reshape(HOLDERS * MAIN, HEAD)
        pre = dot(from_main, mains) + dot(from_tail, tails)
        l_at = jnp.where(place < MAIN, MAIN * k + place, MAIN * PER + TAIL * k + place - MAIN)
        l_pre = jnp.sum(jnp.where(lanes == l_at, l_rows, 0.0), axis=1, keepdims=True)
        l_suf = suft[k, :, 0:1]
        top = jnp.maximum(l_pre, l_suf)
        pre_f, suf_f = jnp.exp2(l_pre - top), jnp.exp2(l_suf - top)
        total = pre_f + suf_f * suft[k, :, 1:2]
        att[0, 0, :, k * HEAD:(k + 1) * HEAD] = (
            (pre * pre_f + sufw[k] * suf_f) / total
        ).astype(BF16)

    piece = rows_n // PIECES

    def rows_of(i):
        return pl.ds(i * piece, piece)

    def hop(way, k, i):
        if way == 0:
            src, dst = (0, 4, 5)[k], k + 1
        else:
            src, dst = k, k + 4
        return to(
            chip[way], att.at[src, 0, rows_of(i)], att.at[dst, 0, rows_of(i)],
            hop_send.at[way, k, i], hop_recv.at[way, k, i],
        )

    def across(b, i):
        return to(
            {"tp": sibling}, att.at[b, 0, rows_of(i)], att.at[b, 1, rows_of(i)],
            core_send.at[b, i], core_recv.at[b, i],
        )

    def weight_of(j, r):
        if j == 0:
            return w_own[r]
        return jnp.concatenate(
            [
                w_far[half, (j - 1) * CORES + r].reshape(q.shape[1], half_out)
                for half in range(HALVES)
            ],
            axis=1,
        )

    def project(b, j):
        return dot(att[b, 0], weight_of(j, 0)) + dot(att[b, 1], weight_of(j, 1))

    def arrived(b):
        for i in range(PIECES):
            across(b, i).wait_recv()

    for i in range(PIECES):
        for way in range(2):
            hop(way, 0, i).start()
    for i in range(PIECES):
        across(0, i).start()
    fetch_own.wait()
    give_own.wait_recv()
    arrived(0)
    acc[0] = project(0, 0)
    for k in range(RING):
        for i in range(PIECES):
            for way in (1, 0):
                if way == 0 and k == RING - 1:
                    continue
                hop(way, k, i).wait_recv()
                if way == 0:
                    hop(1, k + 1, i).start()
                elif k < 2:
                    hop(0, k + 1, i).start()
                across(k + 1 if way == 0 else k + 4, i).start()
        if k == 0:
            ring_wait(1, 0)
            ring_start(1, 1)
            arrived(1)
            acc[1] = project(1, 0)
        if k == 2:
            ring_wait(1, 1)
            for b in (3, 4, 6):
                arrived(b)
            ship[...] = (acc[1] + project(3, 1) + project(4, 3) + project(6, 2)).astype(BF16)
            back_rows = to({"grp": partner}, ship, got, ship_send, ship_recv)
            back_rows.start()
            arrived(2)
            arrived(5)
            acc[0] = acc[0] + project(2, 1) + project(5, 3)
    arrived(7)
    mine = pl.multiple_of(z * pair_out, pair_out)
    other = pl.multiple_of((1 - z) * pair_out, pair_out)
    out[:, pl.ds(mine, pair_out)] = (acc[0] + project(7, 2)).astype(BF16)
    back_rows.wait()
    out[:, pl.ds(other, pair_out)] = got[...]

    def finish(d, carry):
        dispatch(d).wait_send()
        give(d).wait_send()
        give_l(d).wait_send()
        return carry

    lax.fori_loop(1, HOLDERS, finish, 0)
    give_own.wait_send()
    for j, r, half in shares:
        far(j, r, half).wait_send()
    for half, way in ways:
        for second in range(2):
            for stage in range(2):
                ring(half, second, stage, way).wait_send()
    for i in range(PIECES):
        for k in range(RING):
            if k < RING - 1:
                hop(0, k, i).wait_send()
            hop(1, k, i).wait_send()
        for b in range(CHIPS):
            across(b, i).wait_send()


def attend(queries, suffix_kv, cache, weight, readers, owner, lengths):
    rows_n, width = queries.shape
    wide_out = weight.shape[1] // (RING * CORES)
    pair_out = wide_out // NZ
    vmem = pl.BlockSpec(memory_space=pltpu.VMEM)
    smem = pl.BlockSpec(memory_space=pltpu.SMEM)
    sems = pltpu.SemaphoreType.DMA
    dma = sems((HOLDERS,))
    one = sems
    slots = pltpu.VMEM((HOLDERS, SLOT, HEAD), BF16)
    lses = pltpu.VMEM((HOLDERS, 1, HEAD), F32)
    return pl.pallas_call(
        attend_kernel,
        out_shape=jax.ShapeDtypeStruct((rows_n, wide_out), BF16),
        in_specs=[vmem, vmem, vmem, pl.BlockSpec(memory_space=pl.ANY), smem, smem, smem],
        out_specs=vmem,
        scratch_shapes=[
            slots, slots, slots, slots, lses, lses,
            pltpu.VMEM((PER, rows_n, HEAD), F32),
            pltpu.VMEM((PER, rows_n, HEAD), F32),
            pltpu.VMEM((CORES, width, pair_out), BF16),
            pltpu.VMEM(
                (HALVES, (RING - 1) * CORES, NX, NY, SHARE, pair_out // HALVES), BF16
            ),
            pltpu.VMEM((CHIPS, CORES, rows_n, width), BF16),
            pltpu.VMEM((2, rows_n, pair_out), F32),
            pltpu.VMEM((rows_n, pair_out), BF16),
            pltpu.VMEM((rows_n, pair_out), BF16),
            dma, dma, dma, dma, dma, dma,
            one, one, one,
            sems((RING - 1, CORES, HALVES)), sems((RING - 1, CORES, HALVES)),
            sems((HALVES, 2, 2, 2)), sems((HALVES, 2, 2, 2)),
            sems((2, RING, PIECES)), sems((2, RING, PIECES)),
            sems((CHIPS, PIECES)), sems((CHIPS, PIECES)),
            one, one,
        ],
        compiler_params=pltpu.CompilerParams(
            collective_id=0, has_side_effects=True, vmem_limit_bytes=56 * 1024 * 1024
        ),
        cost_estimate=pl.CostEstimate(
            flops=4 * HOLDERS * SLOT * cache.shape[2] * HEAD,
            bytes_accessed=4 * 1024 * 1024,
            transcendentals=HOLDERS * SLOT * cache.shape[2],
        ),
        name="attend",
    )(queries, suffix_kv, cache, weight, readers, owner, lengths)


def local(queries, suffix_kv, prefix_cache, out_weight, readers, owner, lengths):
    return attend(queries, suffix_kv, prefix_cache, out_weight, readers, owner, lengths)


def solution(mesh):
    return jax.shard_map(
        local,
        mesh=mesh,
        in_specs=(
            P("grp", "tp"),
            P("grp", None, "tp"),
            P("grp", None, None, "tp"),
            P("tp", None),
            P("grp", None),
            P(),
            P("grp", None),
        ),
        out_specs=P("grp", "tp"),
        check_vma=False,
    )
```

```python
import math

import jax
import jax.numpy as jnp
from jax import lax
from jax.experimental import pallas as pl
from jax.experimental.pallas import tpu as pltpu
from jax.sharding import PartitionSpec as P

HEAD = 128
MOST = 20
MAIN = 16
TAIL = MOST - MAIN
PER = 4
SLOT = MOST * PER
NX, NY, NZ = 4, 4, 2
HOLDERS = NX * NY * NZ
GROUP = 4
ORDER = (5, 4, 3, 7, 2, 6, 1, 0)
RING = 4
CORES = 2
PIECES = 2
HALVES = 2
CHIPS = RING * NZ
SHARE = 32
NEG = -1e30
FACTOR = math.log2(math.e) / math.sqrt(HEAD)
F32 = jnp.float32
BF16 = jnp.bfloat16


def dot(a, b):
    return jnp.dot(a, b, preferred_element_type=F32)


def dot_t(a, b):
    return lax.dot_general(a, b, (((1,), (1,)), ((), ())), preferred_element_type=F32)


def shifted(x, y, z, d, sign):
    dx, dy, dz = d // (NY * NZ), (d // NZ) % NY, d % NZ
    if sign > 0:
        nx, ny, nz = (x + dx) % NX, (y + dy) % NY, (z + dz) % NZ
    else:
        nx, ny, nz = (x + NX - dx) % NX, (y + NY - dy) % NY, (z + NZ - dz) % NZ
    return nx * (NY * NZ) + ny * NZ + nz


def row_places(shape, axis, me, readers, owner, lengths):
    x, y, z = me
    rows = lax.broadcasted_iota(jnp.int32, shape, axis)
    slot = jnp.zeros(shape, jnp.int32)
    first = jnp.zeros(shape, jnp.int32)
    start = jnp.int32(0)
    for s in range(readers.shape[1]):
        holder = owner[readers[0, s]]
        hx, hy, hz = holder // (NY * NZ), (holder // NZ) % NY, holder % NZ
        d = ((hx + NX - x) % NX) * (NY * NZ) + ((hy + NY - y) % NY) * NZ + (hz + NZ - z) % NZ
        inside = rows >= start
        slot = jnp.where(inside, d, slot)
        first = jnp.where(inside, start, first)
        start = start + lengths[0, s]
    return rows, slot, rows - first, first


def one_hot(cond):
    return jnp.where(cond, 1.0, 0.0).astype(BF16)


def attend_kernel(
    q_in, kv_in, cache_in, weight, readers, owner, lengths, out,
    q, kv, cache, in_sem,
    send, recv, back, ret, lback, lret, sufw, suft,
    w_own, w_far, att, acc, ship, got,
    send_sem, recv_sem, back_sem, ret_sem, lback_sem, lret_sem,
    own_sem, sib_send, sib_recv, far_send, far_recv, ring_send, ring_recv,
    hop_send, hop_recv, core_send, core_recv, ship_send, ship_recv,
):
    me = lax.axis_index("grp")
    x, y, z = me // (NY * NZ), (me // NZ) % NY, me % NZ
    tp = lax.axis_index("tp")
    h, core = tp // CORES, tp % CORES
    sibling = h * CORES + 1 - core
    side = 1 - 2 * z
    partner = x * (NY * NZ) + y * NZ + 1 - z
    outer = (h * NZ + z + CHIPS - side) % CHIPS
    chip = [
        {"grp": partner, "tp": tp},
        {"grp": x * (NY * NZ) + y * NZ + outer % NZ, "tp": (outer // NZ) * CORES + core},
    ]
    rows_n = q.shape[0]
    wide_out = out.shape[1]
    pair_out = wide_out // NZ
    half_out = pair_out // HALVES

    loads = [
        pltpu.make_async_copy(src, dst, in_sem.at[i])
        for i, (src, dst) in enumerate(((q_in, q), (kv_in, kv), (cache_in, cache)))
    ]
    for load in loads:
        load.start()
    barrier = pltpu.get_barrier_semaphore()

    def greet(d, carry):
        pl.semaphore_signal(
            barrier, inc=1, device_id={"grp": shifted(x, y, z, d, 1)},
            device_id_type=pl.DeviceIdType.MESH,
        )
        return carry

    lax.fori_loop(1, HOLDERS, greet, 0)
    for d in range(1, RING * CORES):
        pl.semaphore_signal(
            barrier, inc=1, device_id={"tp": (tp + d) % (RING * CORES)},
            device_id_type=pl.DeviceIdType.MESH,
        )

    pl.semaphore_signal(
        barrier, inc=1, device_id=chip[1], device_id_type=pl.DeviceIdType.MESH
    )

    def columns(b, of_core):
        return pl.multiple_of((b * CORES + of_core) * wide_out + z * pair_out, pair_out)

    def to(device, src, dst, send, recv):
        return pltpu.make_async_remote_copy(
            src_ref=src, dst_ref=dst, send_sem=send, recv_sem=recv,
            device_id=device, device_id_type=pl.DeviceIdType.MESH,
        )

    fetch_own = pltpu.make_async_copy(
        weight.at[:, pl.ds(columns(h, core), pair_out)], w_own.at[0], own_sem
    )
    fetch_own.start()
    give_own = to(
        {"tp": sibling}, weight.at[:, pl.ds(columns(h, 1 - core), pair_out)], w_own.at[1],
        sib_send, sib_recv,
    )
    cores = (core, 1 - core)

    def far(j, r, half):
        target = (h + RING - side * j) % RING
        rows = pl.ds(pl.multiple_of((x * NY + y) * SHARE, SHARE), SHARE)
        first = pl.multiple_of(columns(target, cores[r]) + half * half_out, half_out)
        return to(
            {"tp": target * CORES + cores[r]}, weight.at[rows, pl.ds(first, half_out)],
            w_far.at[half, (j - 1) * CORES + r, x, y],
            far_send.at[j - 1, r, half], far_recv.at[j - 1, r, half],
        )

    def ring(half, second, stage, way):
        step = 1 if way == 0 else 3
        back_by = (3 if way == 0 else 1) * stage
        along_x = (half == 0) == (second == 1)
        if along_x:
            bx, by = (x + back_by) % NX, y
            target = ((x + step) % NX) * (NY * NZ) + y * NZ + z
        else:
            bx, by = x, (y + back_by) % NY
            target = x * (NY * NZ) + ((y + step) % NY) * NZ + z
        some = pl.ds(2 * way, 2)
        if second == 0:
            block = w_far.at[half, :, bx, by]
            if stage == 1:
                block = w_far.at[half, :, bx, by, pl.ds(way * (SHARE // 2), SHARE // 2)]
        elif along_x:
            block = w_far.at[half, :, bx, some] if stage == 1 else w_far.at[half, :, bx]
        else:
            block = w_far.at[half, :, some, by] if stage == 1 else w_far.at[half, :, :, by]
        return to(
            {"grp": target}, block, block,
            ring_send.at[half, second, stage, way], ring_recv.at[half, second, stage, way],
        )

    ways = [(half, way) for half in range(HALVES) for way in range(2)]

    def ring_start(second, stage):
        for half, way in ways:
            ring(half, second, stage, way).start()

    def ring_wait(second, stage):
        for half, way in ways:
            ring(half, second, stage, way).wait_recv()

    shares = [
        (j, r, half) for j in range(1, RING) for r in range(CORES) for half in range(HALVES)
    ]

    loads[0].wait()
    _, slot, place, _ = row_places((1, rows_n), 1, (x, y, z), readers, owner, lengths)
    wide = lax.broadcasted_iota(jnp.int32, (HOLDERS * MAIN, rows_n), 0)
    main_at = jnp.where(place < MAIN, slot * MAIN + place, -1)
    main = dot(one_hot(wide == main_at), q[...]).astype(BF16)
    tail = jnp.zeros((HOLDERS * MAIN, HEAD), F32)
    for k in range(PER):
        cols = slice(k * HEAD, (k + 1) * HEAD)
        send[:, k * MAIN:(k + 1) * MAIN, :] = main[:, cols].reshape(HOLDERS, MAIN, HEAD)
        tail_at = jnp.where(place >= MAIN, slot * MAIN + TAIL * k + place - MAIN, -1)
        tail = tail + dot(one_hot(wide == tail_at), q[:, cols])
    send[:, PER * MAIN:, :] = tail.astype(BF16).reshape(HOLDERS, MAIN, HEAD)

    pl.semaphore_wait(barrier, HOLDERS - 1 + RING * CORES)

    def dispatch(d):
        return pltpu.make_async_remote_copy(
            src_ref=send.at[d], dst_ref=recv.at[d],
            send_sem=send_sem.at[d], recv_sem=recv_sem.at[d],
            device_id={"grp": shifted(x, y, z, d, 1)},
            device_id_type=pl.DeviceIdType.MESH,
        )

    def give(d):
        return pltpu.make_async_remote_copy(
            src_ref=back.at[d], dst_ref=ret.at[d],
            send_sem=back_sem.at[d], recv_sem=ret_sem.at[d],
            device_id={"grp": shifted(x, y, z, d, -1)},
            device_id_type=pl.DeviceIdType.MESH,
        )

    def give_l(d):
        return pltpu.make_async_remote_copy(
            src_ref=lback.at[d], dst_ref=lret.at[d],
            send_sem=lback_sem.at[d], recv_sem=lret_sem.at[d],
            device_id={"grp": shifted(x, y, z, d, -1)},
            device_id_type=pl.DeviceIdType.MESH,
        )

    for a in ORDER:
        for d in range(max(a * GROUP, 1), (a + 1) * GROUP):
            dispatch(d).start()
    recv[0] = send[0]
    give_own.start()

    loads[1].wait()
    loads[2].wait()
    at, slot, place, first = row_places((rows_n, 1), 0, (x, y, z), readers, owner, lengths)
    other = lax.broadcasted_iota(jnp.int32, (rows_n, rows_n), 1)
    visible = (other >= first) & (other <= at)
    keys, values = kv[:, 0, :], kv[:, 1, :]
    for k in range(PER):
        s = dot_t(q[:, k * HEAD:(k + 1) * HEAD], keys)
        s = jnp.where(visible, s, NEG)
        top = jnp.max(s, axis=1, keepdims=True)
        w = jnp.exp2((s - top) * FACTOR)
        total = jnp.sum(w, axis=1, keepdims=True)
        sufw[k] = dot(w.astype(BF16), values)
        suft[k, :, 0:1] = top * FACTOR
        suft[k, :, 1:2] = total

    prefix_keys = cache[0, 0]
    prefix_values = jnp.concatenate(
        [cache[0, 1], jnp.ones((cache.shape[2], HEAD), BF16)], axis=1
    )
    lane = lax.broadcasted_iota(jnp.int32, (SLOT, HEAD), 1)
    sub = lax.broadcasted_iota(jnp.int32, (SLOT, HEAD), 0)
    for turn, a in enumerate(ORDER):
        low = a * GROUP

        for d in range(max(low, 1), low + GROUP):
            dispatch(d).wait_recv()
        block = recv[low:low + GROUP].reshape(GROUP * SLOT, HEAD)
        s = dot_t(block, prefix_keys)
        top = jnp.max(s, axis=1, keepdims=True)
        w = jnp.exp2((s - top) * FACTOR)
        o = dot(w.astype(BF16), prefix_values)
        total = o[:, HEAD:]
        back[low:low + GROUP] = (o[:, :HEAD] / total).astype(BF16).reshape(GROUP, SLOT, HEAD)
        lse = top * FACTOR + jnp.log2(total)
        for i in range(GROUP):
            piece_l = lse[i * SLOT:(i + 1) * SLOT]
            lback[low + i] = jnp.sum(jnp.where(lane == sub, piece_l, 0.0), axis=0, keepdims=True)

        for d in range(max(low, 1), low + GROUP):
            give(d).start()
            give_l(d).start()
        if turn == 0:
            for j, r, half in shares:
                far(j, r, half).start()

    ret[0] = back[0]
    lret[0] = lback[0]

    cols = lax.broadcasted_iota(jnp.int32, (rows_n, HOLDERS * MAIN), 1)
    from_main = one_hot(cols == jnp.where(place < MAIN, slot * MAIN + place, -1))
    slots = lax.broadcasted_iota(jnp.int32, (rows_n, HOLDERS), 1)
    from_slot = one_hot(slots == slot)
    lanes = lax.broadcasted_iota(jnp.int32, (rows_n, HEAD), 1)

    def wait_ret(d, carry):
        give(d).wait_recv()
        give_l(d).wait_recv()
        return carry

    lax.fori_loop(1, HOLDERS, wait_ret, 0)
    for j, r, half in shares:
        far(j, r, half).wait_recv()
    ring_start(0, 0)

    l_all = lret[...].reshape(HOLDERS, HEAD)
    l_high = l_all.astype(BF16)
    l_rest = l_all - l_high.astype(F32)
    l_mid = l_rest.astype(BF16)
    l_low = (l_rest - l_mid.astype(F32)).astype(BF16)
    l_rows = dot(from_slot, l_high) + dot(from_slot, l_mid) + dot(from_slot, l_low)
    tails = ret[:, PER * MAIN:, :].reshape(HOLDERS * MAIN, HEAD)
    for k in range(PER):
        from_tail = one_hot(
            cols == jnp.where(place >= MAIN, slot * MAIN + TAIL * k + place - MAIN, -1)
        )
        mains = ret[:, k * MAIN:(k + 1) * MAIN, :].reshape(HOLDERS * MAIN, HEAD)
        pre = dot(from_main, mains) + dot(from_tail, tails)
        l_at = jnp.where(place < MAIN, MAIN * k + place, MAIN * PER + TAIL * k + place - MAIN)
        l_pre = jnp.sum(jnp.where(lanes == l_at, l_rows, 0.0), axis=1, keepdims=True)
        l_suf = suft[k, :, 0:1]
        top = jnp.maximum(l_pre, l_suf)
        pre_f, suf_f = jnp.exp2(l_pre - top), jnp.exp2(l_suf - top)
        total = pre_f + suf_f * suft[k, :, 1:2]
        att[0, 0, :, k * HEAD:(k + 1) * HEAD] = (
            (pre * pre_f + sufw[k] * suf_f) / total
        ).astype(BF16)

    piece = rows_n // PIECES

    def rows_of(i):
        return pl.ds(i * piece, piece)

    def hop(way, k, i):
        if way == 0:
            src, dst = (0, 4, 5)[k], k + 1
        else:
            src, dst = k, k + 4
        return to(
            chip[way], att.at[src, 0, rows_of(i)], att.at[dst, 0, rows_of(i)],
            hop_send.at[way, k, i], hop_recv.at[way, k, i],
        )

    def across(b, i):
        return to(
            {"tp": sibling}, att.at[b, 0, rows_of(i)], att.at[b, 1, rows_of(i)],
            core_send.at[b, i], core_recv.at[b, i],
        )

    def weight_of(j, r):
        if j == 0:
            return w_own[r]
        return jnp.concatenate(
            [
                w_far[half, (j - 1) * CORES + r].reshape(q.shape[1], half_out)
                for half in range(HALVES)
            ],
            axis=1,
        )

    def project(b, j):
        return dot(att[b, 0], weight_of(j, 0)) + dot(att[b, 1], weight_of(j, 1))

    def arrived(b):
        for i in range(PIECES):
            across(b, i).wait_recv()

    for i in range(PIECES):
        for way in range(2):
            hop(way, 0, i).start()
    for i in range(PIECES):
        across(0, i).start()
    ring_wait(0, 0)
    ring_start(0, 1)
    fetch_own.wait()
    give_own.wait_recv()
    arrived(0)
    acc[0] = project(0, 0)
    for k in range(RING):
        for i in range(PIECES):
            for way in (1, 0):
                if way == 0 and k == RING - 1:
                    continue
                hop(way, k, i).wait_recv()
                if way == 0:
                    hop(1, k + 1, i).start()
                elif k < 2:
                    hop(0, k + 1, i).start()
                across(k + 1 if way == 0 else k + 4, i).start()
        if k == 0:
            ring_wait(0, 1)
            ring_start(1, 0)
            arrived(1)
            acc[1] = project(1, 0)
        if k == 1:
            ring_wait(1, 0)
            ring_start(1, 1)
        if k == 2:
            for b in (3, 4, 6):
                arrived(b)
            ring_wait(1, 1)
            ship[...] = (acc[1] + project(3, 1) + project(4, 3) + project(6, 2)).astype(BF16)
            back_rows = to({"grp": partner}, ship, got, ship_send, ship_recv)
            back_rows.start()
            arrived(2)
            arrived(5)
            acc[0] = acc[0] + project(2, 1) + project(5, 3)
    arrived(7)
    mine = pl.multiple_of(z * pair_out, pair_out)
    other = pl.multiple_of((1 - z) * pair_out, pair_out)
    out[:, pl.ds(mine, pair_out)] = (acc[0] + project(7, 2)).astype(BF16)
    back_rows.wait()
    out[:, pl.ds(other, pair_out)] = got[...]

    def finish(d, carry):
        dispatch(d).wait_send()
        give(d).wait_send()
        give_l(d).wait_send()
        return carry

    lax.fori_loop(1, HOLDERS, finish, 0)
    give_own.wait_send()
    for j, r, half in shares:
        far(j, r, half).wait_send()
    for half, way in ways:
        for second in range(2):
            for stage in range(2):
                ring(half, second, stage, way).wait_send()
    for i in range(PIECES):
        for k in range(RING):
            if k < RING - 1:
                hop(0, k, i).wait_send()
            hop(1, k, i).wait_send()
        for b in range(CHIPS):
            across(b, i).wait_send()


def attend(queries, suffix_kv, cache, weight, readers, owner, lengths):
    rows_n, width = queries.shape
    wide_out = weight.shape[1] // (RING * CORES)
    pair_out = wide_out // NZ
    vmem = pl.BlockSpec(memory_space=pltpu.VMEM)
    smem = pl.BlockSpec(memory_space=pltpu.SMEM)
    anywhere = pl.BlockSpec(memory_space=pl.ANY)
    sems = pltpu.SemaphoreType.DMA
    dma = sems((HOLDERS,))
    one = sems
    slots = pltpu.VMEM((HOLDERS, SLOT, HEAD), BF16)
    lses = pltpu.VMEM((HOLDERS, 1, HEAD), F32)
    return pl.pallas_call(
        attend_kernel,
        out_shape=pltpu.VMEM((rows_n, wide_out), BF16),
        in_specs=[anywhere, anywhere, anywhere, anywhere, smem, smem, smem],
        out_specs=vmem,
        scratch_shapes=[
            pltpu.VMEM(queries.shape, BF16), pltpu.VMEM(suffix_kv.shape, BF16),
            pltpu.VMEM(cache.shape, BF16), sems((3,)),
            slots, slots, slots, slots, lses, lses,
            pltpu.VMEM((PER, rows_n, HEAD), F32),
            pltpu.VMEM((PER, rows_n, HEAD), F32),
            pltpu.VMEM((CORES, width, pair_out), BF16),
            pltpu.VMEM(
                (HALVES, (RING - 1) * CORES, NX, NY, SHARE, pair_out // HALVES), BF16
            ),
            pltpu.VMEM((CHIPS, CORES, rows_n, width), BF16),
            pltpu.VMEM((2, rows_n, pair_out), F32),
            pltpu.VMEM((rows_n, pair_out), BF16),
            pltpu.VMEM((rows_n, pair_out), BF16),
            dma, dma, dma, dma, dma, dma,
            one, one, one,
            sems((RING - 1, CORES, HALVES)), sems((RING - 1, CORES, HALVES)),
            sems((HALVES, 2, 2, 2)), sems((HALVES, 2, 2, 2)),
            sems((2, RING, PIECES)), sems((2, RING, PIECES)),
            sems((CHIPS, PIECES)), sems((CHIPS, PIECES)),
            one, one,
        ],
        compiler_params=pltpu.CompilerParams(
            collective_id=0, has_side_effects=True, vmem_limit_bytes=56 * 1024 * 1024
        ),
        cost_estimate=pl.CostEstimate(
            flops=4 * HOLDERS * SLOT * cache.shape[2] * HEAD,
            bytes_accessed=4 * 1024 * 1024,
            transcendentals=HOLDERS * SLOT * cache.shape[2],
        ),
        name="attend",
    )(queries, suffix_kv, cache, weight, readers, owner, lengths)


def local(queries, suffix_kv, prefix_cache, out_weight, readers, owner, lengths):
    return attend(queries, suffix_kv, prefix_cache, out_weight, readers, owner, lengths)


def solution(mesh):
    return jax.shard_map(
        local,
        mesh=mesh,
        in_specs=(
            P("grp", "tp"),
            P("grp", None, "tp"),
            P("grp", None, None, "tp"),
            P("tp", None),
            P("grp", None),
            P(),
            P("grp", None),
        ),
        out_specs=P("grp", "tp"),
        check_vma=False,
    )
```

```python
import math

import jax
import jax.numpy as jnp
from jax import lax
from jax.experimental import pallas as pl
from jax.experimental.pallas import tpu as pltpu
from jax.sharding import PartitionSpec as P

HEAD = 128
MOST = 20
MAIN = 16
TAIL = MOST - MAIN
PER = 4
SLOT = MOST * PER
NX, NY, NZ = 4, 4, 2
HOLDERS = NX * NY * NZ
GROUP = 4
ORDER = (5, 4, 3, 7, 2, 6, 1, 0)
RING = 4
CORES = 2
PIECES = 2
HALVES = 2
CHIPS = RING * NZ
SHARE = 32
NEG = -1e30
FACTOR = math.log2(math.e) / math.sqrt(HEAD)
F32 = jnp.float32
BF16 = jnp.bfloat16


def dot(a, b):
    return jnp.dot(a, b, preferred_element_type=F32)


def dot_t(a, b):
    return lax.dot_general(a, b, (((1,), (1,)), ((), ())), preferred_element_type=F32)


def offsets(x, y, z):
    return (
        [lax.rem(x + i, NX) * (NY * NZ) for i in range(NX)],
        [lax.rem(y + i, NY) * NZ for i in range(NY)],
        [lax.rem(z + i, NZ) for i in range(NZ)],
    )


def shifted(steps, d, sign):
    dx, dy, dz = d // (NY * NZ), (d // NZ) % NY, d % NZ
    if sign < 0:
        dx, dy, dz = (NX - dx) % NX, (NY - dy) % NY, (NZ - dz) % NZ
    return steps[0][dx] + steps[1][dy] + steps[2][dz]


def row_places(shape, axis, me, readers, owner, lengths):
    x, y, z = me
    rows = lax.broadcasted_iota(jnp.int32, shape, axis)
    slot = jnp.zeros(shape, jnp.int32)
    first = jnp.zeros(shape, jnp.int32)
    start = jnp.int32(0)
    for s in range(readers.shape[1]):
        holder = owner[readers[0, s]]
        hx, hy, hz = holder // (NY * NZ), (holder // NZ) % NY, holder % NZ
        d = ((hx + NX - x) % NX) * (NY * NZ) + ((hy + NY - y) % NY) * NZ + (hz + NZ - z) % NZ
        inside = rows >= start
        slot = jnp.where(inside, d, slot)
        first = jnp.where(inside, start, first)
        start = start + lengths[0, s]
    return rows, slot, rows - first, first


def one_hot(cond):
    return jnp.where(cond, 1.0, 0.0).astype(BF16)


def attend_kernel(
    q_in, kv_in, cache_in, weight, readers, owner, lengths, out,
    q, kv, cache, from_tail, in_sem,
    send, recv, back, ret, lback, lret, sufw, suft,
    w_own, w_far, att, acc, ship, got,
    send_sem, recv_sem, back_sem, ret_sem, lback_sem, lret_sem,
    own_sem, sib_send, sib_recv, far_send, far_recv, ring_send, ring_recv,
    hop_send, hop_recv, core_send, core_recv, ship_send, ship_recv,
):
    me = lax.axis_index("grp")
    x, y, z = me // (NY * NZ), (me // NZ) % NY, me % NZ
    tp = lax.axis_index("tp")
    h, core = tp // CORES, tp % CORES
    sibling = h * CORES + 1 - core
    side = 1 - 2 * z
    partner = x * (NY * NZ) + y * NZ + 1 - z
    outer = (h * NZ + z + CHIPS - side) % CHIPS
    chip = [
        {"grp": partner, "tp": tp},
        {"grp": x * (NY * NZ) + y * NZ + outer % NZ, "tp": (outer // NZ) * CORES + core},
    ]
    steps = offsets(x, y, z)
    rows_n = q.shape[0]
    wide_out = out.shape[1]
    pair_out = wide_out // NZ
    half_out = pair_out // HALVES

    loads = [
        pltpu.make_async_copy(src, dst, in_sem.at[i])
        for i, (src, dst) in enumerate(((q_in, q), (kv_in, kv), (cache_in, cache)))
    ]
    for load in loads:
        load.start()
    barrier = pltpu.get_barrier_semaphore()

    def greet(d):
        pl.semaphore_signal(
            barrier, inc=1, device_id={"grp": shifted(steps, d, 1)},
            device_id_type=pl.DeviceIdType.MESH,
        )

    for d in range(1, HOLDERS):
        greet(d)
    for d in range(1, RING * CORES):
        pl.semaphore_signal(
            barrier, inc=1, device_id={"tp": (tp + d) % (RING * CORES)},
            device_id_type=pl.DeviceIdType.MESH,
        )

    pl.semaphore_signal(
        barrier, inc=1, device_id=chip[1], device_id_type=pl.DeviceIdType.MESH
    )

    def columns(b, of_core):
        return pl.multiple_of((b * CORES + of_core) * wide_out + z * pair_out, pair_out)

    def to(device, src, dst, send, recv):
        return pltpu.make_async_remote_copy(
            src_ref=src, dst_ref=dst, send_sem=send, recv_sem=recv,
            device_id=device, device_id_type=pl.DeviceIdType.MESH,
        )

    fetch_own = pltpu.make_async_copy(
        weight.at[:, pl.ds(columns(h, core), pair_out)], w_own.at[0], own_sem
    )
    fetch_own.start()
    give_own = to(
        {"tp": sibling}, weight.at[:, pl.ds(columns(h, 1 - core), pair_out)], w_own.at[1],
        sib_send, sib_recv,
    )
    cores = (core, 1 - core)

    def far(j, r, half):
        target = (h + RING - side * j) % RING
        rows = pl.ds(pl.multiple_of((x * NY + y) * SHARE, SHARE), SHARE)
        first = columns(target, cores[r])
        return to(
            {"tp": target * CORES + cores[r]}, weight.at[rows, pl.ds(first, pair_out)],
            w_far.at[(j - 1) * CORES + r, x, y],
            far_send.at[j - 1, r, half], far_recv.at[j - 1, r, half],
        )

    def ring(half, second, stage, way):
        step = 1 if way == 0 else 3
        back_by = (3 if way == 0 else 1) * stage
        along_x = (half == 0) == (second == 1)
        if along_x:
            bx, by = (x + back_by) % NX, y
            target = ((x + step) % NX) * (NY * NZ) + y * NZ + z
        else:
            bx, by = x, (y + back_by) % NY
            target = x * (NY * NZ) + ((y + step) % NY) * NZ + z
        some = pl.ds(2 * way, 2)
        cols = pl.ds(half * half_out, half_out)
        if second == 0:
            block = w_far.at[:, bx, by, :, cols]
            if stage == 1:
                block = w_far.at[:, bx, by, pl.ds(way * (SHARE // 2), SHARE // 2), cols]
        elif along_x:
            block = w_far.at[:, bx, some, :, cols] if stage == 1 else w_far.at[:, bx, :, :, cols]
        else:
            block = w_far.at[:, some, by, :, cols] if stage == 1 else w_far.at[:, :, by, :, cols]
        return to(
            {"grp": target}, block, block,
            ring_send.at[half, second, stage, way], ring_recv.at[half, second, stage, way],
        )

    ways = [(half, way) for half in range(HALVES) for way in range(2)]

    def ring_start(second, stage):
        for half, way in ways:
            ring(half, second, stage, way).start()

    def ring_wait(second, stage):
        for half, way in ways:
            ring(half, second, stage, way).wait_recv()

    shares = [
        (j, r, half) for j in range(1, RING) for r in range(CORES) for half in range(1)
    ]

    loads[0].wait()
    _, slot, place, _ = row_places((1, rows_n), 1, (x, y, z), readers, owner, lengths)
    wide = lax.broadcasted_iota(jnp.int32, (HOLDERS * MAIN, rows_n), 0)
    main_at = jnp.where(place < MAIN, slot * MAIN + place, -1)
    main = dot(one_hot(wide == main_at), q[...]).astype(BF16)
    tail = jnp.zeros((HOLDERS * MAIN, HEAD), F32)
    for k in range(PER):
        cols = slice(k * HEAD, (k + 1) * HEAD)
        send[:, k * MAIN:(k + 1) * MAIN, :] = main[:, cols].reshape(HOLDERS, MAIN, HEAD)
        tail_at = jnp.where(place >= MAIN, slot * MAIN + TAIL * k + place - MAIN, -1)
        tail = tail + dot(one_hot(wide == tail_at), q[:, cols])
    send[:, PER * MAIN:, :] = tail.astype(BF16).reshape(HOLDERS, MAIN, HEAD)

    pl.semaphore_wait(barrier, HOLDERS - 1 + RING * CORES)

    def dispatch(d):
        return pltpu.make_async_remote_copy(
            src_ref=send.at[d], dst_ref=recv.at[d],
            send_sem=send_sem.at[d], recv_sem=recv_sem.at[d],
            device_id={"grp": shifted(steps, d, 1)},
            device_id_type=pl.DeviceIdType.MESH,
        )

    def give(d):
        return pltpu.make_async_remote_copy(
            src_ref=back.at[d], dst_ref=ret.at[d],
            send_sem=back_sem.at[d], recv_sem=ret_sem.at[d],
            device_id={"grp": shifted(steps, d, -1)},
            device_id_type=pl.DeviceIdType.MESH,
        )

    def give_l(d):
        return pltpu.make_async_remote_copy(
            src_ref=lback.at[d], dst_ref=lret.at[d],
            send_sem=lback_sem.at[d], recv_sem=lret_sem.at[d],
            device_id={"grp": shifted(steps, d, -1)},
            device_id_type=pl.DeviceIdType.MESH,
        )

    for a in ORDER:
        for d in range(max(a * GROUP, 1), (a + 1) * GROUP):
            dispatch(d).start()
    recv[0] = send[0]
    give_own.start()

    loads[1].wait()
    loads[2].wait()
    at, slot, place, first = row_places((rows_n, 1), 0, (x, y, z), readers, owner, lengths)
    other = lax.broadcasted_iota(jnp.int32, (rows_n, rows_n), 1)
    visible = (other >= first) & (other <= at)
    keys, values = kv[:, 0, :], kv[:, 1, :]
    for k in range(PER):
        s = dot_t(q[:, k * HEAD:(k + 1) * HEAD], keys)
        s = jnp.where(visible, s, NEG)
        top = jnp.max(s, axis=1, keepdims=True)
        w = jnp.exp2((s - top) * FACTOR)
        total = jnp.sum(w, axis=1, keepdims=True)
        sufw[k] = dot(w.astype(BF16), values)
        suft[k, :, 0:1] = top * FACTOR
        suft[k, :, 1:2] = total

    prefix_keys = cache[0, 0]
    prefix_values = jnp.concatenate(
        [cache[0, 1], jnp.ones((cache.shape[2], HEAD), BF16)], axis=1
    )
    lane = lax.broadcasted_iota(jnp.int32, (SLOT, HEAD), 1)
    sub = lax.broadcasted_iota(jnp.int32, (SLOT, HEAD), 0)
    for turn, a in enumerate(ORDER):
        low = a * GROUP

        for d in range(max(low, 1), low + GROUP):
            dispatch(d).wait_recv()
        block = recv[low:low + GROUP].reshape(GROUP * SLOT, HEAD)
        s = dot_t(block, prefix_keys)
        top = jnp.max(s, axis=1, keepdims=True)
        w = jnp.exp2((s - top) * FACTOR)
        o = dot(w.astype(BF16), prefix_values)
        total = o[:, HEAD:]
        back[low:low + GROUP] = (o[:, :HEAD] / total).astype(BF16).reshape(GROUP, SLOT, HEAD)
        lse = top * FACTOR + jnp.log2(total)
        for i in range(GROUP):
            piece_l = lse[i * SLOT:(i + 1) * SLOT]
            lback[low + i] = jnp.sum(jnp.where(lane == sub, piece_l, 0.0), axis=0, keepdims=True)

        for d in range(max(low, 1), low + GROUP):
            give(d).start()
            give_l(d).start()
        if turn == 0:
            for j, r, half in shares:
                far(j, r, half).start()

    ret[0] = back[0]
    lret[0] = lback[0]

    def hop(way, k, i):
        if way == 0:
            src, dst = (0, 4, 5)[k], k + 1
        else:
            src, dst = k, k + 4
        return to(
            chip[way], att.at[src, 0, i], att.at[dst, 0, i],
            hop_send.at[way, k, i], hop_recv.at[way, k, i],
        )

    def across(b, i):
        return to(
            {"tp": sibling}, att.at[b, 0, i], att.at[b, 1, i],
            core_send.at[b, i], core_recv.at[b, i],
        )

    cols = lax.broadcasted_iota(jnp.int32, (rows_n, HOLDERS * MAIN), 1)
    from_main = one_hot(cols == jnp.where(place < MAIN, slot * MAIN + place, -1))
    slots = lax.broadcasted_iota(jnp.int32, (rows_n, HOLDERS), 1)
    from_slot = one_hot(slots == slot)
    lanes = lax.broadcasted_iota(jnp.int32, (rows_n, HEAD), 1)

    for k in range(PER):
        from_tail[k] = one_hot(
            cols == jnp.where(place >= MAIN, slot * MAIN + TAIL * k + place - MAIN, -1)
        )

    for d in range(1, HOLDERS):
        give(d).wait_recv()
        give_l(d).wait_recv()
    for j, r, half in shares:
        far(j, r, half).wait_recv()
    ring_start(0, 0)

    l_all = lret[...].reshape(HOLDERS, HEAD)
    l_high = l_all.astype(BF16)
    l_rest = l_all - l_high.astype(F32)
    l_mid = l_rest.astype(BF16)
    l_low = (l_rest - l_mid.astype(F32)).astype(BF16)
    l_rows = dot(from_slot, l_high) + dot(from_slot, l_mid) + dot(from_slot, l_low)
    tails = ret[:, PER * MAIN:, :].reshape(HOLDERS * MAIN, HEAD)
    for k in range(PER):
        mains = ret[:, k * MAIN:(k + 1) * MAIN, :].reshape(HOLDERS * MAIN, HEAD)
        pre = dot(from_main, mains) + dot(from_tail[k], tails)
        l_at = jnp.where(place < MAIN, MAIN * k + place, MAIN * PER + TAIL * k + place - MAIN)
        l_pre = jnp.sum(jnp.where(lanes == l_at, l_rows, 0.0), axis=1, keepdims=True)
        l_suf = suft[k, :, 0:1]
        top = jnp.maximum(l_pre, l_suf)
        pre_f, suf_f = jnp.exp2(l_pre - top), jnp.exp2(l_suf - top)
        total = pre_f + suf_f * suft[k, :, 1:2]
        i, at_k = k * PIECES // PER, k % (PER // PIECES) * HEAD
        att[0, 0, i, :, at_k:at_k + HEAD] = (
            (pre * pre_f + sufw[k] * suf_f) / total
        ).astype(BF16)
        if (k + 1) % (PER // PIECES) == 0:
            for way in range(2):
                hop(way, 0, i).start()
            across(0, i).start()

    def weight_of(j, r):
        if j == 0:
            return w_own[r]
        return w_far[(j - 1) * CORES + r].reshape(q.shape[1], pair_out)

    def project(b, j):
        rows = [
            jnp.concatenate([att[b, r, i] for i in range(PIECES)], axis=1) for r in range(CORES)
        ]
        return dot(rows[0], weight_of(j, 0)) + dot(rows[1], weight_of(j, 1))

    def arrived(b):
        for i in range(PIECES):
            across(b, i).wait_recv()

    ring_wait(0, 0)
    ring_start(0, 1)
    fetch_own.wait()
    give_own.wait_recv()
    arrived(0)
    acc[0] = project(0, 0)
    for k in range(RING):
        for i in range(PIECES):
            for way in (1, 0):
                if way == 0 and k == RING - 1:
                    continue
                hop(way, k, i).wait_recv()
                if way == 0:
                    hop(1, k + 1, i).start()
                elif k < 2:
                    hop(0, k + 1, i).start()
                across(k + 1 if way == 0 else k + 4, i).start()
        if k == 0:
            for d in range(1, HOLDERS):
                dispatch(d).wait_send()
                give(d).wait_send()
                give_l(d).wait_send()
            give_own.wait_send()
            for j, r, half in shares:
                far(j, r, half).wait_send()
            ring_wait(0, 1)
            ring_start(1, 0)
            arrived(1)
            acc[1] = project(1, 0)
        if k == 1:
            ring_wait(1, 0)
            ring_start(1, 1)
        if k == 2:
            for b in (3, 4, 6):
                arrived(b)
            ring_wait(1, 1)
            ship[...] = (acc[1] + project(3, 1) + project(4, 3) + project(6, 2)).astype(BF16)
            back_rows = to({"grp": partner}, ship, got, ship_send, ship_recv)
            back_rows.start()
            arrived(2)
            arrived(5)
            acc[0] = acc[0] + project(2, 1) + project(5, 3)
            for half, way in ways:
                for second in range(2):
                    for stage in range(2):
                        ring(half, second, stage, way).wait_send()
            for i in range(PIECES):
                for n in range(RING - 1):
                    hop(0, n, i).wait_send()
                for n in range(2):
                    hop(1, n, i).wait_send()
                for b in (0, 1, 2, 4, 5):
                    across(b, i).wait_send()
    arrived(7)
    mine = pl.multiple_of(z * pair_out, pair_out)
    other = pl.multiple_of((1 - z) * pair_out, pair_out)
    out[:, pl.ds(mine, pair_out)] = (acc[0] + project(7, 2)).astype(BF16)
    back_rows.wait()
    out[:, pl.ds(other, pair_out)] = got[...]

    for k in range(2, RING):
        for i in range(PIECES):
            hop(1, k, i).wait_send()
    for i in range(PIECES):
        for b in (3, 6, 7):
            across(b, i).wait_send()


def attend(queries, suffix_kv, cache, weight, readers, owner, lengths):
    rows_n, width = queries.shape
    wide_out = weight.shape[1] // (RING * CORES)
    pair_out = wide_out // NZ
    vmem = pl.BlockSpec(memory_space=pltpu.VMEM)
    smem = pl.BlockSpec(memory_space=pltpu.SMEM)
    anywhere = pl.BlockSpec(memory_space=pl.ANY)
    sems = pltpu.SemaphoreType.DMA
    dma = sems((HOLDERS,))
    one = sems
    slots = pltpu.VMEM((HOLDERS, SLOT, HEAD), BF16)
    lses = pltpu.VMEM((HOLDERS, 1, HEAD), F32)
    return pl.pallas_call(
        attend_kernel,
        out_shape=pltpu.VMEM((rows_n, wide_out), BF16),
        in_specs=[anywhere, anywhere, anywhere, anywhere, smem, smem, smem],
        out_specs=vmem,
        scratch_shapes=[
            pltpu.VMEM(queries.shape, BF16), pltpu.VMEM(suffix_kv.shape, BF16),
            pltpu.VMEM(cache.shape, BF16),
            pltpu.VMEM((PER, rows_n, HOLDERS * MAIN), BF16), sems((3,)),
            slots, slots, slots, slots, lses, lses,
            pltpu.VMEM((PER, rows_n, HEAD), F32),
            pltpu.VMEM((PER, rows_n, HEAD), F32),
            pltpu.VMEM((CORES, width, pair_out), BF16),
            pltpu.VMEM(
                ((RING - 1) * CORES, NX, NY, SHARE, pair_out), BF16
            ),
            pltpu.VMEM((CHIPS, CORES, PIECES, rows_n, width // PIECES), BF16),
            pltpu.VMEM((2, rows_n, pair_out), F32),
            pltpu.VMEM((rows_n, pair_out), BF16),
            pltpu.VMEM((rows_n, pair_out), BF16),
            dma, dma, dma, dma, dma, dma,
            one, one, one,
            sems((RING - 1, CORES, HALVES)), sems((RING - 1, CORES, HALVES)),
            sems((HALVES, 2, 2, 2)), sems((HALVES, 2, 2, 2)),
            sems((2, RING, PIECES)), sems((2, RING, PIECES)),
            sems((CHIPS, PIECES)), sems((CHIPS, PIECES)),
            one, one,
        ],
        compiler_params=pltpu.CompilerParams(
            collective_id=0, has_side_effects=True, vmem_limit_bytes=56 * 1024 * 1024
        ),
        cost_estimate=pl.CostEstimate(
            flops=4 * HOLDERS * SLOT * cache.shape[2] * HEAD,
            bytes_accessed=4 * 1024 * 1024,
            transcendentals=HOLDERS * SLOT * cache.shape[2],
        ),
        name="attend",
    )(queries, suffix_kv, cache, weight, readers, owner, lengths)


def local(queries, suffix_kv, prefix_cache, out_weight, readers, owner, lengths):
    return attend(queries, suffix_kv, prefix_cache, out_weight, readers, owner, lengths)


def solution(mesh):
    return jax.shard_map(
        local,
        mesh=mesh,
        in_specs=(
            P("grp", "tp"),
            P("grp", None, "tp"),
            P("grp", None, None, "tp"),
            P("tp", None),
            P("grp", None),
            P(),
            P("grp", None),
        ),
        out_specs=P("grp", "tp"),
        check_vma=False,
    )
```

```python
import math

import jax
import jax.numpy as jnp
from jax import lax
from jax.experimental import pallas as pl
from jax.experimental.pallas import tpu as pltpu
from jax.sharding import PartitionSpec as P

HEAD = 128
MOST = 20
MAIN = 16
TAIL = MOST - MAIN
PER = 4
SLOT = MOST * PER
NX, NY, NZ = 4, 4, 2
HOLDERS = NX * NY * NZ
GROUP = 4
ORDER = (5, 4, 7, 3, 6, 2, 1, 0)
RING = 4
CORES = 2
PIECES = 2
HALVES = 2
CHIPS = RING * NZ
SHARE = 32
NEG = -1e30
FACTOR = math.log2(math.e) / math.sqrt(HEAD)
F32 = jnp.float32
BF16 = jnp.bfloat16


def dot(a, b):
    return jnp.dot(a, b, preferred_element_type=F32)


def dot_t(a, b):
    return lax.dot_general(a, b, (((1,), (1,)), ((), ())), preferred_element_type=F32)


def offsets(x, y, z):
    return (
        [lax.rem(x + i, NX) * (NY * NZ) for i in range(NX)],
        [lax.rem(y + i, NY) * NZ for i in range(NY)],
        [lax.rem(z + i, NZ) for i in range(NZ)],
    )


def shifted(steps, d, sign):
    dx, dy, dz = d // (NY * NZ), (d // NZ) % NY, d % NZ
    if sign < 0:
        dx, dy, dz = (NX - dx) % NX, (NY - dy) % NY, (NZ - dz) % NZ
    return steps[0][dx] + steps[1][dy] + steps[2][dz]


def row_places(shape, axis, me, readers, owner, lengths):
    x, y, z = me
    rows = lax.broadcasted_iota(jnp.int32, shape, axis)
    slot = jnp.zeros(shape, jnp.int32)
    first = jnp.zeros(shape, jnp.int32)
    start = jnp.int32(0)
    for s in range(readers.shape[1]):
        holder = owner[readers[0, s]]
        hx, hy, hz = holder // (NY * NZ), (holder // NZ) % NY, holder % NZ
        d = ((hx + NX - x) % NX) * (NY * NZ) + ((hy + NY - y) % NY) * NZ + (hz + NZ - z) % NZ
        inside = rows >= start
        slot = jnp.where(inside, d, slot)
        first = jnp.where(inside, start, first)
        start = start + lengths[0, s]
    return rows, slot, rows - first, first


def one_hot(cond):
    return jnp.where(cond, 1.0, 0.0).astype(BF16)


def attend_kernel(
    q_in, kv_in, cache_in, weight, readers, owner, lengths, out,
    q, kv, cache, from_tail, in_sem,
    send, recv, back, ret, sufw, suft,
    w_own, w_far, att, acc, ship, got,
    send_sem, recv_sem, back_sem, ret_sem,
    own_sem, sib_send, sib_recv, far_send, far_recv, ring_send, ring_recv,
    hop_send, hop_recv, core_send, core_recv, ship_send, ship_recv,
):
    me = lax.axis_index("grp")
    x, y, z = me // (NY * NZ), (me // NZ) % NY, me % NZ
    tp = lax.axis_index("tp")
    h, core = tp // CORES, tp % CORES
    sibling = h * CORES + 1 - core
    side = 1 - 2 * z
    partner = x * (NY * NZ) + y * NZ + 1 - z
    outer = (h * NZ + z + CHIPS - side) % CHIPS
    chip = [
        {"grp": partner, "tp": tp},
        {"grp": x * (NY * NZ) + y * NZ + outer % NZ, "tp": (outer // NZ) * CORES + core},
    ]
    steps = offsets(x, y, z)
    rows_n = q.shape[0]
    wide_out = out.shape[1]
    pair_out = wide_out // NZ
    half_out = pair_out // HALVES

    loads = [
        pltpu.make_async_copy(src, dst, in_sem.at[i])
        for i, (src, dst) in enumerate(((q_in, q), (kv_in, kv), (cache_in, cache)))
    ]
    for load in loads:
        load.start()
    barrier = pltpu.get_barrier_semaphore()

    def greet(d):
        pl.semaphore_signal(
            barrier, inc=1, device_id={"grp": shifted(steps, d, 1)},
            device_id_type=pl.DeviceIdType.MESH,
        )

    for d in range(1, HOLDERS):
        greet(d)
    for d in range(1, RING * CORES):
        pl.semaphore_signal(
            barrier, inc=1, device_id={"tp": (tp + d) % (RING * CORES)},
            device_id_type=pl.DeviceIdType.MESH,
        )

    pl.semaphore_signal(
        barrier, inc=1, device_id=chip[1], device_id_type=pl.DeviceIdType.MESH
    )

    def columns(b, of_core):
        return pl.multiple_of((b * CORES + of_core) * wide_out + z * pair_out, pair_out)

    def to(device, src, dst, send, recv):
        return pltpu.make_async_remote_copy(
            src_ref=src, dst_ref=dst, send_sem=send, recv_sem=recv,
            device_id=device, device_id_type=pl.DeviceIdType.MESH,
        )

    fetch_own = pltpu.make_async_copy(
        weight.at[:, pl.ds(columns(h, core), pair_out)], w_own.at[0], own_sem
    )
    fetch_own.start()
    give_own = to(
        {"tp": sibling}, weight.at[:, pl.ds(columns(h, 1 - core), pair_out)], w_own.at[1],
        sib_send, sib_recv,
    )
    cores = (core, 1 - core)

    def far(j, r, half):
        target = (h + RING - side * j) % RING
        rows = pl.ds(pl.multiple_of((x * NY + y) * SHARE, SHARE), SHARE)
        first = columns(target, cores[r])
        return to(
            {"tp": target * CORES + cores[r]}, weight.at[rows, pl.ds(first, pair_out)],
            w_far.at[(j - 1) * CORES + r, x, y],
            far_send.at[j - 1, r, half], far_recv.at[j - 1, r, half],
        )

    def ring(half, second, stage, way):
        step = 1 if way == 0 else 3
        back_by = (3 if way == 0 else 1) * stage
        along_x = (half == 0) == (second == 1)
        if along_x:
            bx, by = (x + back_by) % NX, y
            target = ((x + step) % NX) * (NY * NZ) + y * NZ + z
        else:
            bx, by = x, (y + back_by) % NY
            target = x * (NY * NZ) + ((y + step) % NY) * NZ + z
        some = pl.ds(2 * way, 2)
        cols = pl.ds(half * half_out, half_out)
        if second == 0:
            block = w_far.at[:, bx, by, :, cols]
            if stage == 1:
                block = w_far.at[:, bx, by, pl.ds(way * (SHARE // 2), SHARE // 2), cols]
        elif along_x:
            block = w_far.at[:, bx, some, :, cols] if stage == 1 else w_far.at[:, bx, :, :, cols]
        else:
            block = w_far.at[:, some, by, :, cols] if stage == 1 else w_far.at[:, :, by, :, cols]
        return to(
            {"grp": target}, block, block,
            ring_send.at[half, second, stage, way], ring_recv.at[half, second, stage, way],
        )

    ways = [(half, way) for half in range(HALVES) for way in range(2)]

    def ring_start(second, stage):
        for half, way in ways:
            ring(half, second, stage, way).start()

    def ring_wait(second, stage):
        for half, way in ways:
            ring(half, second, stage, way).wait_recv()

    shares = [
        (j, r, half) for j in range(1, RING) for r in range(CORES) for half in range(1)
    ]

    loads[0].wait()
    _, slot, place, _ = row_places((1, rows_n), 1, (x, y, z), readers, owner, lengths)
    wide = lax.broadcasted_iota(jnp.int32, (HOLDERS * MAIN, rows_n), 0)
    main_at = jnp.where(place < MAIN, slot * MAIN + place, -1)
    main = dot(one_hot(wide == main_at), q[...]).astype(BF16)
    tail = jnp.zeros((HOLDERS * MAIN, HEAD), F32)
    for k in range(PER):
        cols = slice(k * HEAD, (k + 1) * HEAD)
        send[:, k * MAIN:(k + 1) * MAIN, :] = main[:, cols].reshape(HOLDERS, MAIN, HEAD)
        tail_at = jnp.where(place >= MAIN, slot * MAIN + TAIL * k + place - MAIN, -1)
        tail = tail + dot(one_hot(wide == tail_at), q[:, cols])
    send[:, PER * MAIN:, :] = tail.astype(BF16).reshape(HOLDERS, MAIN, HEAD)

    pl.semaphore_wait(barrier, HOLDERS - 1 + RING * CORES)

    def dispatch(d):
        return pltpu.make_async_remote_copy(
            src_ref=send.at[d], dst_ref=recv.at[d],
            send_sem=send_sem.at[d], recv_sem=recv_sem.at[d],
            device_id={"grp": shifted(steps, d, 1)},
            device_id_type=pl.DeviceIdType.MESH,
        )

    def give(d):
        return pltpu.make_async_remote_copy(
            src_ref=back.at[d], dst_ref=ret.at[d],
            send_sem=back_sem.at[d], recv_sem=ret_sem.at[d],
            device_id={"grp": shifted(steps, d, -1)},
            device_id_type=pl.DeviceIdType.MESH,
        )

    for a in ORDER:
        for d in range(max(a * GROUP, 1), (a + 1) * GROUP):
            dispatch(d).start()
    recv[0] = send[0]
    give_own.start()

    loads[1].wait()
    loads[2].wait()
    at, slot, place, first = row_places((rows_n, 1), 0, (x, y, z), readers, owner, lengths)
    other = lax.broadcasted_iota(jnp.int32, (rows_n, rows_n), 1)
    visible = (other >= first) & (other <= at)
    keys, values = kv[:, 0, :], kv[:, 1, :]
    for k in range(PER):
        s = dot_t(q[:, k * HEAD:(k + 1) * HEAD], keys)
        s = jnp.where(visible, s, NEG)
        top = jnp.max(s, axis=1, keepdims=True)
        w = jnp.exp2((s - top) * FACTOR)
        total = jnp.sum(w, axis=1, keepdims=True)
        sufw[k] = dot(w.astype(BF16), values)
        suft[k, :, 0:1] = top * FACTOR
        suft[k, :, 1:2] = total

    prefix_keys = cache[0, 0]
    prefix_values = jnp.concatenate(
        [cache[0, 1], jnp.ones((cache.shape[2], HEAD), BF16)], axis=1
    )
    lane = lax.broadcasted_iota(jnp.int32, (SLOT, HEAD), 1)
    sub = lax.broadcasted_iota(jnp.int32, (SLOT, HEAD), 0)
    l_sub = lax.broadcasted_iota(jnp.int32, (MAIN, HEAD), 0)
    for turn, a in enumerate(ORDER):
        low = a * GROUP

        for d in range(max(low, 1), low + GROUP):
            dispatch(d).wait_recv()
        block = recv[low:low + GROUP].reshape(GROUP * SLOT, HEAD)
        s = dot_t(block, prefix_keys)
        top = jnp.max(s, axis=1, keepdims=True)
        w = jnp.exp2((s - top) * FACTOR)
        o = dot(w.astype(BF16), prefix_values)
        total = o[:, HEAD:]
        back[low:low + GROUP, :SLOT] = (o[:, :HEAD] / total).astype(BF16).reshape(GROUP, SLOT, HEAD)
        lse = top * FACTOR + jnp.log2(total)
        for i in range(GROUP):
            piece_l = lse[i * SLOT:(i + 1) * SLOT]
            l_row = jnp.sum(jnp.where(lane == sub, piece_l, 0.0), axis=0, keepdims=True)
            l_high = l_row.astype(BF16).astype(F32)
            l_mid = (l_row - l_high).astype(BF16).astype(F32)
            l_low = l_row - l_high - l_mid
            l_block = jnp.where(
                l_sub == 0, l_high, jnp.where(l_sub == 1, l_mid, jnp.where(l_sub == 2, l_low, 0.0))
            )
            back[low + i, SLOT:] = l_block.astype(BF16)

        for d in range(max(low, 1), low + GROUP):
            give(d).start()
        if turn == 0:
            for j, r, half in shares:
                far(j, r, half).start()

    ret[0] = back[0]

    def hop(way, k, i):
        if way == 0:
            src, dst = (0, 4, 5)[k], k + 1
        else:
            src, dst = k, k + 4
        return to(
            chip[way], att.at[src, 0, i], att.at[dst, 0, i],
            hop_send.at[way, k, i], hop_recv.at[way, k, i],
        )

    def across(b, i):
        return to(
            {"tp": sibling}, att.at[b, 0, i], att.at[b, 1, i],
            core_send.at[b, i], core_recv.at[b, i],
        )

    cols = lax.broadcasted_iota(jnp.int32, (rows_n, HOLDERS * MAIN), 1)
    from_main = one_hot(cols == jnp.where(place < MAIN, slot * MAIN + place, -1))
    from_slot = one_hot((cols >= slot * MAIN) & (cols < slot * MAIN + 3))
    lanes = lax.broadcasted_iota(jnp.int32, (rows_n, HEAD), 1)

    for k in range(PER):
        from_tail[k] = one_hot(
            cols == jnp.where(place >= MAIN, slot * MAIN + TAIL * k + place - MAIN, -1)
        )

    for d in range(1, HOLDERS):
        give(d).wait_recv()
    for j, r, half in shares:
        far(j, r, half).wait_recv()
    ring_start(0, 0)

    l_rows = dot(from_slot, ret[:, SLOT:, :].reshape(HOLDERS * MAIN, HEAD))
    tails = ret[:, PER * MAIN:SLOT, :].reshape(HOLDERS * MAIN, HEAD)
    for k in range(PER):
        mains = ret[:, k * MAIN:(k + 1) * MAIN, :].reshape(HOLDERS * MAIN, HEAD)
        pre = dot(from_main, mains) + dot(from_tail[k], tails)
        l_at = jnp.where(place < MAIN, MAIN * k + place, MAIN * PER + TAIL * k + place - MAIN)
        l_pre = jnp.sum(jnp.where(lanes == l_at, l_rows, 0.0), axis=1, keepdims=True)
        l_suf = suft[k, :, 0:1]
        top = jnp.maximum(l_pre, l_suf)
        pre_f, suf_f = jnp.exp2(l_pre - top), jnp.exp2(l_suf - top)
        total = pre_f + suf_f * suft[k, :, 1:2]
        i, at_k = k * PIECES // PER, k % (PER // PIECES) * HEAD
        att[0, 0, i, :, at_k:at_k + HEAD] = (
            (pre * pre_f + sufw[k] * suf_f) / total
        ).astype(BF16)
        if (k + 1) % (PER // PIECES) == 0:
            for way in range(2):
                hop(way, 0, i).start()
            across(0, i).start()

    def weight_of(j, r):
        if j == 0:
            return w_own[r]
        return w_far[(j - 1) * CORES + r].reshape(q.shape[1], pair_out)

    def project(b, j):
        rows = [
            jnp.concatenate([att[b, r, i] for i in range(PIECES)], axis=1) for r in range(CORES)
        ]
        return dot(rows[0], weight_of(j, 0)) + dot(rows[1], weight_of(j, 1))

    def arrived(b):
        for i in range(PIECES):
            across(b, i).wait_recv()

    ring_wait(0, 0)
    ring_start(0, 1)
    fetch_own.wait()
    give_own.wait_recv()
    arrived(0)
    acc[0] = project(0, 0)
    for k in range(RING):
        for i in range(PIECES):
            for way in (1, 0):
                if way == 0 and k == RING - 1:
                    continue
                hop(way, k, i).wait_recv()
                if way == 0:
                    hop(1, k + 1, i).start()
                elif k < 2:
                    hop(0, k + 1, i).start()
                across(k + 1 if way == 0 else k + 4, i).start()
        if k == 0:
            for d in range(1, HOLDERS):
                dispatch(d).wait_send()
                give(d).wait_send()
            give_own.wait_send()
            for j, r, half in shares:
                far(j, r, half).wait_send()
            ring_wait(0, 1)
            ring_start(1, 0)
            arrived(1)
            acc[1] = project(1, 0)
        if k == 1:
            ring_wait(1, 0)
            ring_start(1, 1)
        if k == 2:
            for b in (3, 4, 6):
                arrived(b)
            ring_wait(1, 1)
            ship[...] = (acc[1] + project(3, 1) + project(4, 3) + project(6, 2)).astype(BF16)
            back_rows = to({"grp": partner}, ship, got, ship_send, ship_recv)
            back_rows.start()
            arrived(2)
            arrived(5)
            acc[0] = acc[0] + project(2, 1) + project(5, 3)
            for half, way in ways:
                for second in range(2):
                    for stage in range(2):
                        ring(half, second, stage, way).wait_send()
            for i in range(PIECES):
                for n in range(RING - 1):
                    hop(0, n, i).wait_send()
                for n in range(2):
                    hop(1, n, i).wait_send()
                for b in (0, 1, 2, 4, 5):
                    across(b, i).wait_send()
    arrived(7)
    mine = pl.multiple_of(z * pair_out, pair_out)
    other = pl.multiple_of((1 - z) * pair_out, pair_out)
    out[:, pl.ds(mine, pair_out)] = (acc[0] + project(7, 2)).astype(BF16)
    back_rows.wait()
    out[:, pl.ds(other, pair_out)] = got[...]

    for k in range(2, RING):
        for i in range(PIECES):
            hop(1, k, i).wait_send()
    for i in range(PIECES):
        for b in (3, 6, 7):
            across(b, i).wait_send()


def attend(queries, suffix_kv, cache, weight, readers, owner, lengths):
    rows_n, width = queries.shape
    wide_out = weight.shape[1] // (RING * CORES)
    pair_out = wide_out // NZ
    vmem = pl.BlockSpec(memory_space=pltpu.VMEM)
    smem = pl.BlockSpec(memory_space=pltpu.SMEM)
    anywhere = pl.BlockSpec(memory_space=pl.ANY)
    sems = pltpu.SemaphoreType.DMA
    dma = sems((HOLDERS,))
    one = sems
    slots = pltpu.VMEM((HOLDERS, SLOT, HEAD), BF16)
    results = pltpu.VMEM((HOLDERS, SLOT + MAIN, HEAD), BF16)
    return pl.pallas_call(
        attend_kernel,
        out_shape=pltpu.VMEM((rows_n, wide_out), BF16),
        in_specs=[anywhere, anywhere, anywhere, anywhere, smem, smem, smem],
        out_specs=vmem,
        scratch_shapes=[
            pltpu.VMEM(queries.shape, BF16), pltpu.VMEM(suffix_kv.shape, BF16),
            pltpu.VMEM(cache.shape, BF16),
            pltpu.VMEM((PER, rows_n, HOLDERS * MAIN), BF16), sems((3,)),
            slots, slots, results, results,
            pltpu.VMEM((PER, rows_n, HEAD), F32),
            pltpu.VMEM((PER, rows_n, HEAD), F32),
            pltpu.VMEM((CORES, width, pair_out), BF16),
            pltpu.VMEM(
                ((RING - 1) * CORES, NX, NY, SHARE, pair_out), BF16
            ),
            pltpu.VMEM((CHIPS, CORES, PIECES, rows_n, width // PIECES), BF16),
            pltpu.VMEM((2, rows_n, pair_out), F32),
            pltpu.VMEM((rows_n, pair_out), BF16),
            pltpu.VMEM((rows_n, pair_out), BF16),
            dma, dma, dma, dma,
            one, one, one,
            sems((RING - 1, CORES, HALVES)), sems((RING - 1, CORES, HALVES)),
            sems((HALVES, 2, 2, 2)), sems((HALVES, 2, 2, 2)),
            sems((2, RING, PIECES)), sems((2, RING, PIECES)),
            sems((CHIPS, PIECES)), sems((CHIPS, PIECES)),
            one, one,
        ],
        compiler_params=pltpu.CompilerParams(
            collective_id=0, has_side_effects=True, vmem_limit_bytes=56 * 1024 * 1024
        ),
        cost_estimate=pl.CostEstimate(
            flops=4 * HOLDERS * SLOT * cache.shape[2] * HEAD,
            bytes_accessed=4 * 1024 * 1024,
            transcendentals=HOLDERS * SLOT * cache.shape[2],
        ),
        name="attend",
    )(queries, suffix_kv, cache, weight, readers, owner, lengths)


def local(queries, suffix_kv, prefix_cache, out_weight, readers, owner, lengths):
    return attend(queries, suffix_kv, prefix_cache, out_weight, readers, owner, lengths)


def solution(mesh):
    return jax.shard_map(
        local,
        mesh=mesh,
        in_specs=(
            P("grp", "tp"),
            P("grp", None, "tp"),
            P("grp", None, None, "tp"),
            P("tp", None),
            P("grp", None),
            P(),
            P("grp", None),
        ),
        out_specs=P("grp", "tp"),
        check_vma=False,
    )
```
